32 devices in a mesh: rep: 4 (over x, core), grp: 8 (over z, y).
Axes of the slice: x: 2, y: 2, z: 4, core: 2. Of those that a mesh axis runs over, the one named last changes fastest.
Arguments:
- tokens: bfloat16 [4, 1024, 2048], P('rep', 'grp'), may hold values from -6 to 6
- q_weight: bfloat16 [2048, 2048], P('grp'), may hold values from -0.125 to 0.125
- k_weight: bfloat16 [2048, 2048], P('grp'), may hold values from -0.125 to 0.125
- v_weight: bfloat16 [2048, 2048], P('grp'), may hold values from -0.125 to 0.125
- o_weight: bfloat16 [2048, 2048], P('grp'), may hold values from -0.125 to 0.125
- gate_weight: bfloat16 [2048, 8192], P('grp'), may hold values from -0.125 to 0.125
- up_weight: bfloat16 [2048, 8192], P('grp'), may hold values from -0.125 to 0.125
- down_weight: bfloat16 [8192, 2048], P(None, 'grp'), may hold values from -0.0625 to 0.0625
- q_gain: bfloat16 [2048], P('grp'), may hold values from 0.5 to 1.5
- k_gain: bfloat16 [2048], P('grp'), may hold values from 0.5 to 1.5
- attn_gain: bfloat16 [2048], P('grp'), may hold values from 0.5 to 1.5
- mlp_gain: bfloat16 [2048], P('grp'), may hold values from 0.5 to 1.5
- cotangent: bfloat16 [4, 1024, 2048], P('rep', 'grp'), may hold values from -6 to 6
Outputs:
- outputs: bfloat16 [4, 1024, 2048], P('rep', 'grp')
- d_tokens: bfloat16 [4, 1024, 2048], P('rep', 'grp')
- q_grad: float32 [2048, 2048], P('grp')
- k_grad: float32 [2048, 2048], P('grp')
- v_grad: float32 [2048, 2048], P('grp')
- o_grad: float32 [2048, 2048], P('grp')
- gate_grad: float32 [2048, 8192], P('grp')
- up_grad: float32 [2048, 8192], P('grp')
- down_grad: float32 [8192, 2048], P(None, 'grp')
- q_gain_grad: float32 [2048], P('grp')
- k_gain_grad: float32 [2048], P('grp')
- attn_gain_grad: float32 [2048], P('grp')
- mlp_gain_grad: float32 [2048], P('grp')
The draws below stay inside these ranges and needn't reach their ends.
All inputs are finite; a program needn't handle non-finite values.
Results may differ from the reference program's by a relative error of at most 0.017.
Values may be sent and summed in bfloat16 or wider, within the bound.
No kernel may reach another device: no remote copies, remote signals or barrier semaphores. Data moves between devices by JAX's collectives and lax.ppermute only.
A program may use at most 640 MiB of HBM per device.

```python
import math
import jax
import jax.numpy as jnp
from jax import lax

D = 2048
HEADS = 16
HEAD = 128
FF = 8192
SEQS = 4
LENGTH = 1024


def block_scale(key, dims, pieces, least, largest):
    gain, own = 1.0, jax.random.fold_in(key, 6)
    for position, parts in pieces:
        steps = jnp.exp(jax.random.uniform(jax.random.fold_in(own, position), (parts,), jnp.float32, least / len(pieces), largest / len(pieces)))
        gain = gain * jnp.repeat(steps, dims[position] // parts).reshape([-1 if axis == position else 1 for axis in range(len(dims))])
    return gain


def centred(stream_key, extent, width, most, split=(), kind=jnp.bfloat16):
    array = jax.random.normal(stream_key, extent, jnp.float32) * width
    if len(split) > 0:
        array = block_scale(stream_key, extent, split, -0.22, 0.18) * array
    return jnp.clip(array, min=-most, max=most).astype(kind)


def setup_inputs(seed: int = 0) -> dict:
    key_list = jax.random.split(jax.random.key(seed), 14)
    tokens = centred(key_list[0], (SEQS, LENGTH, D), 1.0, 6.0, ((0, 4), (1, 8)))
    q_weight = centred(key_list[1], (D, D), D ** -0.5, 0.125, ((0, 8),))
    k_weight = centred(key_list[2], (D, D), D ** -0.5, 0.125, ((0, 8),))
    v_weight = centred(key_list[3], (D, D), D ** -0.5, 0.125, ((0, 8),))
    o_weight = centred(key_list[4], (D, D), D ** -0.5, 0.125, ((0, 8),))
    gate_weight = centred(key_list[5], (D, FF), D ** -0.5, 0.125, ((0, 8),))
    up_weight = centred(key_list[6], (D, FF), D ** -0.5, 0.125, ((0, 8),))
    down_weight = centred(key_list[7], (FF, D), FF ** -0.5, 0.0625, ((1, 8),))
    q_gain = jnp.clip(1.0 + 0.1 * jax.random.normal(key_list[8], (D,), jnp.float32), 0.5, 1.5).astype(jnp.bfloat16)
    k_gain = jnp.clip(1.0 + 0.1 * jax.random.normal(key_list[9], (D,), jnp.float32), 0.5, 1.5).astype(jnp.bfloat16)
    attn_gain = jnp.clip(1.0 + 0.1 * jax.random.normal(key_list[10], (D,), jnp.float32), 0.5, 1.5).astype(jnp.bfloat16)
    mlp_gain = jnp.clip(1.0 + 0.1 * jax.random.normal(key_list[11], (D,), jnp.float32), 0.5, 1.5).astype(jnp.bfloat16)
    cotangent = centred(key_list[12], (SEQS, LENGTH, D), 1.0, 6.0, ((0, 4), (1, 8)))
    return {"tokens": tokens, "q_weight": q_weight, "k_weight": k_weight, "v_weight": v_weight, "o_weight": o_weight, "gate_weight": gate_weight, "up_weight": up_weight, "down_weight": down_weight, "q_gain": q_gain, "k_gain": k_gain, "attn_gain": attn_gain, "mlp_gain": mlp_gain, "cotangent": cotangent}


@jax.custom_vjp
def low(v):
    return lax.optimization_barrier(v.astype(jnp.bfloat16)).astype(jnp.float32)

@jax.custom_vjp
def low_back(v):
    return v

def low_keep(v):
    return (low(v), None)

def low_pass(kept, grad):
    return (grad,)

def back_keep(v):
    return (v, None)

def back_low(kept, grad):
    return (low(grad),)
low.defvjp(low_keep, low_pass)
low_back.defvjp(back_keep, back_low)
EPS = 1e-06
THETA = 500000.0
HIGH = lax.Precision.HIGHEST

def rms_scale(values, gains):
    return values * lax.rsqrt(lax.optimization_barrier(jnp.mean(values * values, axis=-1, keepdims=True)) + EPS) * gains

def rotary(values, places):
    count = values.shape[0]
    heads = values.reshape(count, HEADS, HEAD)
    freqs = THETA ** (-2.0 * jnp.arange(HEAD // 2, dtype=jnp.float32) / HEAD)
    angles = places[:, None] * freqs[None, :]
    cosine = jnp.cos(angles)[:, None, :]
    sine = jnp.sin(angles)[:, None, :]
    first = heads[..., :HEAD // 2]
    second = heads[..., HEAD // 2:]
    turned = jnp.concatenate([first * cosine - second * sine, second * cosine + first * sine], axis=-1)
    return turned.reshape(count, HEADS * HEAD)

def attend(queries, keys_in, values_in):
    length = queries.shape[0]
    block = math.gcd(length, 512)
    count = length // block
    query_heads = queries.reshape(count, block, HEADS, HEAD)
    key_heads = keys_in.reshape(length, HEADS, HEAD)
    value_heads = values_in.reshape(length, HEADS, HEAD)
    key_places = jnp.arange(length, dtype=jnp.int32)
    scale = HEAD ** (-0.5)

    @jax.checkpoint
    def one_block(inputs):
        query_block, index = inputs
        raw_scores = jnp.einsum('qhd,khd->hqk', query_block, key_heads, precision=HIGH)
        scores = low_back(raw_scores * scale)
        query_places = index * block + jnp.arange(block, dtype=jnp.int32)
        allowed = key_places[None, :] <= query_places[:, None]
        scores = jnp.where(allowed[None], scores, -1e+30)
        top_score = lax.optimization_barrier(jnp.max(scores, axis=-1, keepdims=True))
        weights = jnp.exp(scores - top_score)
        probs = low(weights / lax.optimization_barrier(jnp.sum(weights, axis=-1, keepdims=True)))
        return jnp.einsum('hqk,khd->qhd', probs, value_heads, precision=HIGH)
    mixed = lax.map(one_block, (query_heads, jnp.arange(count, dtype=jnp.int32)))
    return mixed.reshape(length, HEADS * HEAD)

def layer(inputs, wq_full, wk_full, wv_full, wo_full, wg_full, wu_full, wd_full, gq_full, gk_full, ga_full, gm_full):
    places = jnp.arange(inputs.shape[0], dtype=jnp.int32).astype(jnp.float32)
    q_proj = low_back(jnp.dot(inputs, wq_full, precision=HIGH))
    k_proj = low_back(jnp.dot(inputs, wk_full, precision=HIGH))
    values_bf = low(low_back(jnp.dot(inputs, wv_full, precision=HIGH)))
    queries = low(rotary(rms_scale(q_proj, gq_full), places))
    keys_rot = low(rotary(rms_scale(k_proj, gk_full), places))
    attn_bf = low(low_back(attend(queries, keys_rot, values_bf)))
    a_proj = low_back(jnp.dot(attn_bf, wo_full, precision=HIGH))
    middle = inputs + rms_scale(a_proj, ga_full)
    middle_bf = low(middle)
    gates = low_back(jnp.dot(middle_bf, wg_full, precision=HIGH))
    uppers = low_back(jnp.dot(middle_bf, wu_full, precision=HIGH))
    hidden = low(jax.nn.silu(gates) * uppers)
    y_proj = low_back(jnp.dot(hidden, wd_full, precision=HIGH))
    return middle + rms_scale(y_proj, gm_full)

def reference(tokens, q_weight, k_weight, v_weight, o_weight, gate_weight, up_weight, down_weight, q_gain, k_gain, attn_gain, mlp_gain, cotangent):
    params = tuple((item.astype(jnp.float32) for item in (q_weight, k_weight, v_weight, o_weight, gate_weight, up_weight, down_weight, q_gain, k_gain, attn_gain, mlp_gain)))

    def one_sequence(totals, inputs):
        sequence, grad_out = inputs
        result, pull_back = jax.vjp(layer, sequence.astype(jnp.float32), *params)
        grad_list = pull_back(grad_out.astype(jnp.float32))
        totals = tuple((left + right for left, right in zip(totals, grad_list[1:])))
        return (totals, (result.astype(jnp.bfloat16), grad_list[0].astype(jnp.bfloat16)))
    initial = tuple((jnp.zeros_like(item) for item in params))
    totals, (outputs, d_tokens) = lax.scan(one_sequence, initial, (tokens, cotangent))
    return (outputs, d_tokens, totals[0], totals[1], totals[2], totals[3], totals[4], totals[5], totals[6], totals[7], totals[8], totals[9], totals[10])
```

```python
import jax
import jax.numpy as jnp
from jax import lax
from jax.sharding import PartitionSpec as P

HEADS = 16
HEAD = 128
EPS = 1e-06
THETA = 500000.0
GROUPED = 4
BF = jnp.bfloat16
F32 = jnp.float32


def dot(left, right, dims=((1,), (0,)), kind=F32):
    return lax.dot_general(left, right, (dims, ((), ())), preferred_element_type=kind)


def dot_right_t(left, right):
    return dot(left, right, ((1,), (1,)))


def dot_left_t(left, right):
    return dot(left, right, ((0,), (0,)))


def shuffle(value, axis, step):
    return lax.ppermute(value, axis, [(i, i ^ step) for i in range(lax.axis_size(axis))])


def gather_pieces(value):
    count = lax.axis_size("grp")
    pieces = [None] * count
    pieces[0] = value
    for step in range(count - 2, 0, -2):
        pieces[step] = shuffle(value, "grp", step)
    for step in [0, *range(count - 2, 0, -2)]:
        pieces[step + 1] = shuffle(pieces[step], "grp", 1)
    return pieces


def scatter_sum(pieces):
    count = len(pieces)
    order = [*range(count - 2, -1, -2)]
    moved = {step: shuffle(pieces[step + 1].astype(BF), "grp", 1) for step in order}
    total = None
    for step in order:
        paired = pieces[step].astype(F32) + moved[step].astype(F32)
        if step:
            paired = shuffle(paired.astype(BF), "grp", step).astype(F32)
        total = paired if total is None else total + paired
    return total


def exchange(pieces):
    return [pieces[0]] + [shuffle(pieces[k], "grp", k) for k in range(1, len(pieces))]


def group_sum(value):
    step = 1
    while step < lax.axis_size("grp"):
        value = value + shuffle(value, "grp", step)
        step *= 2
    return value


def across_rep(value):
    far = shuffle(value, "rep", 2)
    return [value, shuffle(value, "rep", 1), far, shuffle(far, "rep", 1)]


def rep_sum(parts):
    near = [
        (parts[j].astype(F32) + shuffle(parts[j ^ 1].astype(BF), "rep", 1).astype(F32)) for j in (0, 2)
    ]
    return (near[0] + shuffle(near[1].astype(BF), "rep", 2).astype(F32)).astype(BF)


def put(buffer, part, starts):
    return lax.dynamic_update_slice(buffer, part, starts)


def rms(values, gains):
    return values * lax.rsqrt(jnp.mean(values * values, axis=-1, keepdims=True) + EPS) * gains


def angles_of(count):
    freqs = THETA ** (-2.0 * jnp.arange(HEAD // 2, dtype=F32) / HEAD)
    angles = jnp.arange(count, dtype=jnp.int32).astype(F32)[:, None] * freqs[None, :]
    return jnp.cos(angles), jnp.sin(angles)


def turn(values, cosine, sine):
    half = HEAD // 2
    out = []
    for start in range(0, values.shape[1], HEAD):
        first, second = values[:, start : start + half], values[:, start + half : start + HEAD]
        out += [first * cosine - second * sine, second * cosine + first * sine]
    return jnp.concatenate(out, axis=1)


def swiglu(gates, uppers):
    return jax.nn.silu(gates) * uppers


def attend(queries, keys, values):
    length = queries.shape[0]
    split = lambda a: a.reshape(length, -1, HEAD)
    scores = jnp.einsum("qhd,khd->hqk", split(queries), split(keys), preferred_element_type=F32)
    scores = scores * HEAD ** (-0.5)
    places = jnp.arange(length, dtype=jnp.int32)
    scores = jnp.where((places[None, :] <= places[:, None])[None], scores, -1e30)
    top = jnp.max(scores, axis=-1, keepdims=True)
    weights = jnp.exp(scores - top)
    totals = jnp.sum(weights, axis=-1, keepdims=True)
    probs = (weights / totals).astype(BF)
    mixed = jnp.einsum("hqk,khd->qhd", probs, split(values), preferred_element_type=F32)
    return mixed.reshape(length, -1).astype(BF), top + jnp.log(totals)


def attend_back(queries, keys, values, lse, grads):
    length = queries.shape[0]
    split = lambda a: a.reshape(length, -1, HEAD)
    scale = HEAD ** (-0.5)
    q, k, v, do = split(queries), split(keys), split(values), split(grads)
    scores = jnp.einsum("qhd,khd->hqk", q, k, preferred_element_type=F32) * scale
    places = jnp.arange(length, dtype=jnp.int32)
    scores = jnp.where((places[None, :] <= places[:, None])[None], scores, -1e30)
    probs = jnp.exp(scores - lse)
    d_probs = jnp.einsum("qhd,khd->hqk", do, v, preferred_element_type=F32)
    delta = jnp.sum(probs * d_probs, axis=-1, keepdims=True)
    ds = (probs * (d_probs - delta)).astype(BF)
    dv = jnp.einsum("hqk,qhd->khd", probs.astype(BF), do, preferred_element_type=F32)
    dq = jnp.einsum("hqk,khd->qhd", ds, k, preferred_element_type=F32) * scale
    dk = jnp.einsum("hqk,qhd->khd", ds, q, preferred_element_type=F32) * scale
    return dq.reshape(length, -1), dk.reshape(length, -1), dv.reshape(length, -1)


def by_heads(
    tokens, q_weight, k_weight, v_weight, o_weight, gate_weight, up_weight, down_weight,
    q_gain, k_gain, attn_gain, mlp_gain, cotangent,
):
    x = tokens[0]
    count, width = x.shape
    groups = lax.axis_size("grp")
    reps = 4
    me, rep = lax.axis_index("grp"), lax.axis_index("rep")
    length = count * groups
    own = width // groups
    hidden = gate_weight.shape[1]
    block = hidden // groups
    part = block // reps
    sub = own // reps
    zero = jnp.int32(0)
    at = [me ^ k for k in range(groups)]
    of = [rep ^ j for j in range(reps)]

    sends = [
        jnp.concatenate(
            [lax.dynamic_slice(w, (rep * sub, at[k] * own), (sub, own)) for w in (q_weight, k_weight, v_weight)],
            axis=1,
        )
        for k in range(groups)
    ]
    landed = jnp.zeros((groups, sub, 3 * own), BF)
    for k, piece in enumerate(exchange(sends)):
        landed = put(landed, piece[None], (at[k], zero, zero))
    w_qkv = jnp.zeros((groups, reps, sub, 3 * own), BF)
    for j, piece in enumerate(across_rep(landed)):
        w_qkv = put(w_qkv, piece[:, None], (zero, of[j], zero, zero))
    w_qkv = w_qkv.reshape(width, 3 * own)

    x_all = jnp.zeros((groups, count, width), BF)
    for k, piece in enumerate(gather_pieces(x)):
        x_all = put(x_all, piece[None], (at[k], zero, zero))
    x_all = x_all.reshape(length, width)

    stripe = width // reps
    gains = jnp.concatenate([attn_gain, mlp_gain])
    gains = jnp.pad(gains[None], ((0, 15), (0, stripe - 2 * own)))
    o_part = jnp.concatenate([lax.dynamic_slice(o_weight, (zero, rep * stripe), (own, stripe)), gains])
    o_mine = jnp.zeros((groups, own, stripe), BF)
    gain_all = jnp.zeros((groups, 2, own), BF)
    for k, piece in enumerate(gather_pieces(o_part)):
        o_mine = put(o_mine, piece[None, :own], (at[k], zero, zero))
        gain_all = put(gain_all, piece[own, : 2 * own].reshape(1, 2, own), (at[k], zero, zero))
    w_o = jnp.zeros((width, width), BF)
    for j, piece in enumerate(across_rep(o_mine.reshape(width, stripe))):
        w_o = put(w_o, piece, (zero, of[j] * stripe))
    ga = gain_all[:, 0].reshape(width).astype(F32)
    gm = gain_all[:, 1].reshape(width).astype(F32)

    sends = []
    for k in range(groups):
        start = at[k] * block + rep * part
        sends.append(
            jnp.concatenate(
                [
                    lax.dynamic_slice(gate_weight, (zero, start), (own, part)),
                    lax.dynamic_slice(up_weight, (zero, start), (own, part)),
                    lax.dynamic_slice(down_weight, (start, zero), (part, own)).T,
                ],
                axis=1,
            )
        )
    landed_gu = jnp.zeros((groups, own, 2 * part), BF)
    landed_d = jnp.zeros((groups, own, part), BF)
    for k, piece in enumerate(exchange(sends)):
        landed_gu = put(landed_gu, piece[None, :, : 2 * part], (at[k], zero, zero))
        landed_d = put(landed_d, piece[None, :, 2 * part :], (at[k], zero, zero))
    gu_parts = across_rep(landed_gu.reshape(width, 2 * part))
    d_parts = across_rep(landed_d.reshape(width, part))
    w_gu = jnp.concatenate([p[:, :part] for p in gu_parts] + [p[:, part:] for p in gu_parts], axis=1)
    w_d = jnp.concatenate(d_parts, axis=1)

    gq, gk = q_gain.astype(F32), k_gain.astype(F32)
    cosine, sine = angles_of(length)
    qkv = dot(x_all, w_qkv)
    q_proj, k_proj = qkv[:, :own], qkv[:, own : 2 * own]
    values = qkv[:, 2 * own :].astype(BF)
    squares = jnp.stack([jnp.sum(q_proj * q_proj, axis=1), jnp.sum(k_proj * k_proj, axis=1)])
    squares = group_sum(squares)
    q_inv = lax.rsqrt(squares[0] / width + EPS)[:, None]
    k_inv = lax.rsqrt(squares[1] / width + EPS)[:, None]
    queries = turn(q_proj * q_inv * gq, cosine, sine).astype(BF)
    keys = turn(k_proj * k_inv * gk, cosine, sine).astype(BF)
    attn, lse = attend(queries, keys, values)
    attn_tok = lax.all_to_all(attn, "grp", 0, 1, tiled=True)
    a_proj = dot(attn_tok, w_o)
    middle = x.astype(F32) + rms(a_proj, ga)
    middle_bf = middle.astype(BF)

    h_all = jnp.concatenate(gather_pieces(middle_bf))
    gu = dot(h_all, w_gu)
    gates, uppers = gu[:, :block], gu[:, block:]
    mixed = swiglu(gates, uppers).astype(BF)
    y_part = dot_right_t(mixed, w_d).reshape(groups, count, width)
    y_proj = scatter_sum([y_part[k] for k in range(groups)])
    outputs = (middle + rms(y_proj, gm)).astype(BF)

    grad_out = cotangent[0].astype(F32)
    _, pull = jax.vjp(rms, y_proj, gm)
    dy, d_mlp_gain = pull(grad_out)
    dy_all = jnp.concatenate(gather_pieces(dy.astype(BF)))
    d_mixed = dot(dy_all, w_d)
    _, pull = jax.vjp(swiglu, gates, uppers)
    d_gu = jnp.concatenate([v.astype(BF) for v in pull(d_mixed)], axis=1)
    m_part = dot_right_t(d_gu, w_gu).reshape(groups, count, width)
    d_middle = grad_out + scatter_sum([m_part[k] for k in range(groups)])

    g_gu = dot_left_t(h_all, d_gu).astype(BF)
    g_d = dot_left_t(dy_all, mixed).astype(BF)
    sums = rep_sum(
        [
            jnp.concatenate(
                [
                    g_gu[:, j * part : (j + 1) * part],
                    g_gu[:, block + j * part : block + (j + 1) * part],
                    g_d[:, j * part : (j + 1) * part],
                ],
                axis=1,
            )
            for j in range(reps)
        ]
    ).reshape(groups, own, 3 * part)
    sends = [lax.dynamic_slice(sums, (at[k], zero, zero), (1, own, 3 * part))[0] for k in range(groups)]
    g_mlp = jnp.zeros((groups, own, 3 * part), BF)
    for k, piece in enumerate(exchange(sends)):
        g_mlp = put(g_mlp, piece[None], (at[k], zero, zero))
    g_mlp = jnp.stack(across_rep(lax.optimization_barrier(g_mlp)))
    g_mlp = jnp.concatenate([lax.dynamic_slice(g_mlp, (of[j], zero, zero, zero), (1, groups, own, 3 * part)) for j in range(reps)])
    gate_grad = jnp.transpose(g_mlp[..., :part], (2, 1, 0, 3)).reshape(own, hidden).astype(F32)
    up_grad = jnp.transpose(g_mlp[..., part : 2 * part], (2, 1, 0, 3)).reshape(own, hidden).astype(F32)
    down_grad = jnp.transpose(g_mlp[..., 2 * part :], (1, 0, 3, 2)).reshape(hidden, own).astype(F32)

    _, pull = jax.vjp(rms, a_proj, ga)
    da, d_attn_gain = pull(d_middle)
    da_bf = da.astype(BF)
    d_attn = lax.all_to_all(dot_right_t(da_bf, w_o).astype(BF), "grp", 1, 0, tiled=True)
    dq, dk, dv = attend_back(queries, keys, values, lse, d_attn)
    dq, dk = turn(dq, cosine, -sine), turn(dk, cosine, -sine)
    q_unit, k_unit = q_proj * q_inv, k_proj * k_inv
    d_q_gain, d_k_gain = jnp.sum(dq * q_unit, axis=0), jnp.sum(dk * k_unit, axis=0)
    dq, dk = dq * gq, dk * gk
    along = jnp.concatenate(
        [jnp.sum(dq * q_unit, axis=1), jnp.sum(dk * k_unit, axis=1), d_attn_gain, d_mlp_gain]
    )
    along = group_sum(along.reshape(-1, 128)).reshape(-1)
    q_mean, k_mean = along[:length, None] / width, along[length : 2 * length, None] / width
    d_qkv = jnp.concatenate(
        [
            (q_inv * (dq - q_unit * q_mean)).astype(BF),
            (k_inv * (dk - k_unit * k_mean)).astype(BF),
            dv.astype(BF),
        ],
        axis=1,
    )
    x_part = dot_right_t(d_qkv, w_qkv)
    d_x = d_middle + scatter_sum(
        [lax.dynamic_slice(x_part, (at[k] * count, zero), (count, width)) for k in range(groups)]
    )

    da_all = jnp.zeros((groups, count, width), BF)
    for k, piece in enumerate(gather_pieces(da_bf)):
        da_all = put(da_all, piece[None], (at[k], zero, zero))
    g_o = dot_left_t(attn, da_all.reshape(length, width)).astype(BF)
    o_sum = rep_sum([lax.dynamic_slice(g_o, (zero, of[j] * stripe), (own, stripe)) for j in range(reps)])
    o_grad = jnp.zeros((own, width), F32)
    for j, piece in enumerate(across_rep(lax.optimization_barrier(o_sum))):
        o_grad = put(o_grad, piece.astype(F32), (zero, of[j] * stripe))
    g_qkv = dot_left_t(x_all, d_qkv).astype(BF).reshape(groups, reps, sub, 3 * own)
    sums = rep_sum(
        [lax.dynamic_slice(g_qkv, (zero, of[j], zero, zero), (groups, 1, sub, 3 * own))[:, 0] for j in range(reps)]
    )
    sends = [lax.dynamic_slice(sums, (at[k], zero, zero), (1, sub, 3 * own))[0] for k in range(groups)]
    landed = jnp.zeros((groups, sub, 3 * own), BF)
    for k, piece in enumerate(exchange(sends)):
        landed = put(landed, piece[None], (at[k], zero, zero))
    g_qkv = jnp.zeros((reps, groups, sub, 3 * own), BF)
    for j, piece in enumerate(across_rep(lax.optimization_barrier(landed))):
        g_qkv = put(g_qkv, piece[None], (of[j], zero, zero, zero))
    q_grad, k_grad, v_grad = (
        jnp.transpose(g_qkv[..., i * own : (i + 1) * own], (0, 2, 1, 3)).reshape(own, width).astype(F32)
        for i in range(3)
    )

    post = lax.dynamic_slice(along[2 * length :].reshape(2, width), (zero, me * own), (2, own))
    gain_sums = lax.psum(jnp.concatenate([jnp.stack([d_q_gain, d_k_gain]), post]), "rep")
    return (
        outputs[None], d_x.astype(BF)[None], q_grad, k_grad, v_grad, o_grad, gate_grad, up_grad, down_grad,
        gain_sums[0], gain_sums[1], gain_sums[2], gain_sums[3],
    )


def rotary(values, places):
    count = values.shape[0]
    heads = values.reshape(count, HEADS, HEAD)
    freqs = THETA ** (-2.0 * jnp.arange(HEAD // 2, dtype=jnp.float32) / HEAD)
    angles = places[:, None] * freqs[None, :]
    cosine = jnp.cos(angles)[:, None, :]
    sine = jnp.sin(angles)[:, None, :]
    first = heads[..., : HEAD // 2]
    second = heads[..., HEAD // 2 :]
    turned = jnp.concatenate(
        [first * cosine - second * sine, second * cosine + first * sine], axis=-1
    )
    return turned.reshape(count, HEADS * HEAD)


def head_slice(matrix, index):
    piece = lax.dynamic_slice_in_dim(matrix, index * GROUPED * HEAD, GROUPED * HEAD, 1)
    return piece.reshape(matrix.shape[0], GROUPED, HEAD)


def heads_back(stacked, count):
    return jnp.moveaxis(stacked, 0, 1).reshape(count, HEADS * HEAD)


def by_tokens(
    tokens,
    q_weight,
    k_weight,
    v_weight,
    o_weight,
    gate_weight,
    up_weight,
    down_weight,
    q_gain,
    k_gain,
    attn_gain,
    mlp_gain,
    cotangent,
):
    inputs = tokens[0]
    rows = inputs.shape[0]
    width = inputs.shape[1]
    groups = lax.axis_size("grp")
    length = rows * groups
    query_places = lax.axis_index("grp") * rows + jnp.arange(rows, dtype=jnp.int32)
    places = query_places.astype(jnp.float32)
    scale = HEAD ** (-0.5)
    group_ids = jnp.arange(HEADS // GROUPED, dtype=jnp.int32)
    wq_fwd, wk_fwd, wv_fwd, wo_gathered, gq_bf, gk_bf, ga_bf = (
        lax.all_gather(q_weight, "grp", axis=0, tiled=True),
        lax.all_gather(k_weight, "grp", axis=0, tiled=True),
        lax.all_gather(v_weight, "grp", axis=0, tiled=True),
        lax.all_gather(o_weight, "grp", axis=0, tiled=True),
        lax.all_gather(q_gain, "grp", axis=0, tiled=True),
        lax.all_gather(k_gain, "grp", axis=0, tiled=True),
        lax.all_gather(attn_gain, "grp", axis=0, tiled=True),
    )
    gq_full = gq_bf.astype(jnp.float32)
    gk_full = gk_bf.astype(jnp.float32)
    ga_full = ga_bf.astype(jnp.float32)
    q_proj = dot(inputs, wq_fwd)
    k_proj = dot(inputs, wk_fwd)
    v_proj = dot(inputs, wv_fwd)

    def turn_query(values, gains):
        return rotary(rms(values, gains), places)

    queries = turn_query(q_proj, gq_full).astype(jnp.bfloat16)
    keys_own = turn_query(k_proj, gk_full).astype(jnp.bfloat16)
    values_own = v_proj.astype(jnp.bfloat16)
    keys_all, values_all = (
        lax.all_gather(keys_own, "grp", axis=0, tiled=True),
        lax.all_gather(values_own, "grp", axis=0, tiled=True),
    )
    allowed = jnp.arange(length, dtype=jnp.int32)[None, :] <= query_places[:, None]

    def forward_group(index):
        scores = (
            jnp.einsum(
                "qhd,khd->hqk",
                head_slice(queries, index),
                head_slice(keys_all, index),
                preferred_element_type=jnp.float32,
            )
            * scale
        )
        scores = jnp.where(allowed[None], scores, -1e30)
        top_score = jnp.max(scores, axis=-1, keepdims=True)
        weights = jnp.exp(scores - top_score)
        totals = jnp.sum(weights, axis=-1, keepdims=True)
        probs = (weights / totals).astype(jnp.bfloat16)
        mixed = jnp.einsum(
            "hqk,khd->qhd", probs, head_slice(values_all, index), preferred_element_type=jnp.float32
        )
        return (mixed, (top_score + jnp.log(totals))[..., 0])

    mixed_all, log_totals = lax.map(forward_group, group_ids)
    log_totals = log_totals.reshape(HEADS, rows)
    attn_bf = heads_back(mixed_all, rows).astype(jnp.bfloat16)
    a_proj = dot(attn_bf, wo_gathered)
    middle = inputs.astype(jnp.float32) + rms(a_proj, ga_full)
    middle_bf = middle.astype(jnp.bfloat16)
    wg_fwd, wu_fwd, gm_bf = (
        lax.all_gather(gate_weight, "grp", axis=0, tiled=True),
        lax.all_gather(up_weight, "grp", axis=0, tiled=True),
        lax.all_gather(mlp_gain, "grp", axis=0, tiled=True),
    )
    gm_full = gm_bf.astype(jnp.float32)
    gates = dot(middle_bf, wg_fwd)
    uppers = dot(middle_bf, wu_fwd)
    hidden = swiglu(gates, uppers).astype(jnp.bfloat16)
    y_proj = dot(hidden, lax.all_gather(down_weight, "grp", axis=1, tiled=True))
    outputs = (middle + rms(y_proj, gm_full)).astype(jnp.bfloat16)
    grad_out = cotangent[0].astype(jnp.float32)
    unused_y, pull_mlp = jax.vjp(rms, y_proj, gm_full)
    dy_proj, d_mlp_gain = pull_mlp(grad_out)
    dy_bf = dy_proj.astype(jnp.bfloat16)
    down_full = lax.all_gather(down_weight, "grp", axis=1, tiled=True)
    d_hidden = dot_right_t(dy_bf, down_full)
    unused_h, pull_act = jax.vjp(swiglu, gates, uppers)
    d_gates, d_uppers = pull_act(d_hidden)
    dg_bf = d_gates.astype(jnp.bfloat16)
    du_bf = d_uppers.astype(jnp.bfloat16)
    block = dot_right_t(
        dg_bf, lax.all_gather(gate_weight, "grp", axis=0, tiled=True)
    ) + dot_right_t(du_bf, lax.all_gather(up_weight, "grp", axis=0, tiled=True))
    d_middle = grad_out + block
    unused_a, pull_attn = jax.vjp(rms, a_proj, ga_full)
    da_proj, d_attn_gain = pull_attn(d_middle)
    da_bf = da_proj.astype(jnp.bfloat16)
    wq_full, wk_full, wv_full, wo_full = (
        lax.all_gather(q_weight, "grp", axis=0, tiled=True),
        lax.all_gather(k_weight, "grp", axis=0, tiled=True),
        lax.all_gather(v_weight, "grp", axis=0, tiled=True),
        lax.all_gather(o_weight, "grp", axis=0, tiled=True),
    )
    d_attn_bf = dot_right_t(da_bf, wo_full).astype(jnp.bfloat16)

    def query_group(index):
        query_g = head_slice(queries, index)
        key_g = head_slice(keys_all, index)
        dout_g = head_slice(d_attn_bf, index)
        lse_g = lax.dynamic_slice_in_dim(log_totals, index * GROUPED, GROUPED, 0)
        scores = (
            jnp.einsum("qhd,khd->hqk", query_g, key_g, preferred_element_type=jnp.float32) * scale
        )
        scores = jnp.where(allowed[None], scores, -1e30)
        probs = jnp.exp(scores - lse_g[..., None])
        d_probs = jnp.einsum(
            "qhd,khd->hqk",
            dout_g,
            head_slice(values_all, index),
            preferred_element_type=jnp.float32,
        )
        deltas = jnp.sum(probs * d_probs, axis=-1, keepdims=True)
        ds_bf = (probs * (d_probs - deltas)).astype(jnp.bfloat16)
        d_query = (
            jnp.einsum("hqk,khd->qhd", ds_bf, key_g, preferred_element_type=jnp.float32) * scale
        )
        return (d_query, deltas[..., 0])

    d_query_all, delta_all = lax.map(query_group, group_ids)
    d_queries = heads_back(d_query_all, rows)
    delta_all = delta_all.reshape(HEADS, rows)
    key_places = jnp.arange(rows * lax.axis_size("grp"), dtype=jnp.int32)
    permit = key_places[None, :] <= query_places[:, None]

    def key_group(index):
        query_g = head_slice(queries, index)
        dout_g = head_slice(d_attn_bf, index)
        lse_g = lax.dynamic_slice_in_dim(log_totals, index * GROUPED, GROUPED, 0)
        delta_g = lax.dynamic_slice_in_dim(delta_all, index * GROUPED, GROUPED, 0)
        scores = (
            jnp.einsum(
                "qhd,khd->hqk",
                query_g,
                head_slice(keys_all, index),
                preferred_element_type=jnp.float32,
            )
            * scale
        )
        scores = jnp.where(permit[None], scores, -1e30)
        probs = jnp.exp(scores - lse_g[..., None])
        d_value = jnp.einsum(
            "hqk,qhd->khd", probs.astype(jnp.bfloat16), dout_g, preferred_element_type=jnp.float32
        )
        d_probs = jnp.einsum(
            "qhd,khd->hqk",
            dout_g,
            head_slice(values_all, index),
            preferred_element_type=jnp.float32,
        )
        ds_bf = (probs * (d_probs - delta_g[..., None])).astype(jnp.bfloat16)
        d_key = (
            jnp.einsum("hqk,qhd->khd", ds_bf, query_g, preferred_element_type=jnp.float32) * scale
        )
        return (d_key, d_value)

    d_key_all, d_value_all = lax.map(key_group, group_ids)
    key_grads = lax.psum_scatter(
        jnp.concatenate(
            [
                heads_back(d_key_all, rows * lax.axis_size("grp")),
                heads_back(d_value_all, rows * lax.axis_size("grp")),
            ],
            axis=1,
        ),
        "grp",
        scatter_dimension=0,
        tiled=True,
    )
    dv_bf = key_grads[:, width:].astype(jnp.bfloat16)
    unused_q, pull_query = jax.vjp(turn_query, q_proj, gq_full)
    dq_proj, d_q_gain = pull_query(d_queries)
    unused_k, pull_key = jax.vjp(turn_query, k_proj, gk_full)
    dk_proj, d_k_gain = pull_key(key_grads[:, :width])
    dq_bf = dq_proj.astype(jnp.bfloat16)
    dk_bf = dk_proj.astype(jnp.bfloat16)
    d_inputs = (
        d_middle
        + dot_right_t(dq_bf, wq_full)
        + dot_right_t(dk_bf, wk_full)
        + dot_right_t(dv_bf, wv_full)
    )
    owned_rows = width // groups
    pairs = (
        (inputs, dq_bf), (inputs, dk_bf), (inputs, dv_bf), (attn_bf, da_bf),
        (middle_bf, dg_bf), (middle_bf, du_bf), (dy_bf, hidden),
    )
    weight_sums = []
    for left, right in pairs:
        if weight_sums:
            left, right, weight_sums[-1] = lax.optimization_barrier((left, right, weight_sums[-1]))
        share = lax.psum_scatter(dot_left_t(left, right), "grp", scatter_dimension=0, tiled=True)
        weight_sums.append(lax.psum(share, "rep"))
    gain_stack = jnp.stack([d_q_gain, d_k_gain, d_attn_gain, d_mlp_gain])
    gain_total = lax.psum(gain_stack, ("rep", "grp"))
    gain_mine = lax.dynamic_slice_in_dim(
        gain_total, lax.axis_index("grp") * owned_rows, owned_rows, 1
    )
    return (
        outputs[None],
        d_inputs.astype(jnp.bfloat16)[None],
        *weight_sums[:6],
        weight_sums[6].T,
        gain_mine[0],
        gain_mine[1],
        gain_mine[2],
        gain_mine[3],
    )


def solution(mesh):
    rows = P("grp", None)
    seq = P("rep", "grp", None)
    gain = P("grp")
    whole_heads = HEADS % mesh.shape["grp"] == 0 and mesh.shape["rep"] == 4
    return jax.shard_map(
        by_heads if whole_heads else by_tokens,
        mesh=mesh,
        in_specs=(seq, *[rows] * 6, P(None, "grp"), *[gain] * 4, seq),
        out_specs=(seq, seq, *[rows] * 6, P(None, "grp"), *[gain] * 4),
        check_vma=False,
    )
```

```python
import jax
import jax.numpy as jnp
from jax import lax
from jax.experimental import pallas as pl
from jax.experimental.pallas import tpu as pltpu
from jax.sharding import PartitionSpec as P

HEADS = 16
HEAD = 128
EPS = 1e-06
THETA = 500000.0
GROUPED = 4
BF = jnp.bfloat16
F32 = jnp.float32


def dot(left, right, dims=((1,), (0,)), kind=F32):
    return lax.dot_general(left, right, (dims, ((), ())), preferred_element_type=kind)


def dot_right_t(left, right):
    return dot(left, right, ((1,), (1,)))


def dot_left_t(left, right):
    return dot(left, right, ((0,), (0,)))


def shuffle(value, axis, step):
    return lax.ppermute(value, axis, [(i, i ^ step) for i in range(lax.axis_size(axis))])


def tie(value, *others):
    return lax.optimization_barrier((value, *others))[0]


def gather_pieces(value, *meanwhile):
    count = lax.axis_size("grp")
    top = count - 2
    pieces = [None] * count
    pieces[0] = value
    pieces[top] = shuffle(value, "grp", top)
    for step in range(2, count // 2, 2):
        pieces[step] = shuffle(value, "grp", step)
    pieces[1] = shuffle(value, "grp", 1)
    for step in range(count // 2, top, 2):
        pieces[step] = shuffle(pieces[top], "grp", step ^ top)
    steps = [*range(2, count // 2, 2), top, *range(count // 2, top, 2)]
    for step in steps:
        held = meanwhile if step == steps[-1] else ()
        pieces[step + 1] = shuffle(tie(pieces[step], *held) if held else pieces[step], "grp", 1)
    return pieces


def scatter_sum(pieces, *meanwhile):
    steps = [*range(len(pieces) - 2, 0, -2)]
    cut = pieces[0].shape[1] * 3 // 4
    left = [p[:, :cut] for p in pieces]
    right = [p[:, cut:] for p in pieces]
    odd = shuffle(jnp.stack([left[k + 1].astype(BF) for k in steps]), "grp", 1)
    far = [shuffle(jnp.stack([right[k].astype(BF), right[k + 1].astype(BF)]), "grp", k) for k in steps]
    paired = [left[k].astype(F32) + odd[i].astype(F32) for i, k in enumerate(steps)]
    moved = [shuffle(p.astype(BF), "grp", k) for p, k in zip(paired, steps)]
    both = [right[i].astype(F32) + sum(f[i].astype(F32) for f in far) for i in (0, 1)]
    last = jnp.concatenate([left[1].astype(BF), both[1].astype(BF)], axis=1)
    last = shuffle(tie(last, *meanwhile) if meanwhile else last, "grp", 1)
    total_left = left[0].astype(F32) + sum(m.astype(F32) for m in moved)
    return jnp.concatenate([total_left, both[0]], axis=1) + last.astype(F32), last


def to_columns(blocks):
    return lax.all_to_all(blocks, "grp", 0, 0, tiled=True)


def group_sum(value):
    step = 1
    while step < lax.axis_size("grp"):
        value = value + shuffle(value, "grp", step)
        step *= 2
    return value


def rep_near(value):
    return shuffle(value, "rep", 1)


def rep_far(value):
    return shuffle(value, "rep", 2)


def near_send(parts):
    return rep_near(jnp.stack([parts[1], parts[3]]))


def far_send(parts, near):
    return rep_far((parts[2].astype(F32) + near[1].astype(F32)).astype(BF))


def rep_total(parts, near, far):
    return (parts[0].astype(F32) + near[0].astype(F32) + far.astype(F32)).astype(BF)


def lay_kernel(rep_ref, here_ref, there_ref, *out_refs):
    del rep_ref
    wide = here_ref.shape[3] // len(out_refs)
    here = pl.program_id(0) % 2 == 0
    for i, out_ref in enumerate(out_refs):
        for g in range(here_ref.shape[1]):
            piece = jnp.where(
                here,
                here_ref[0, g, :, i * wide : (i + 1) * wide].astype(F32),
                there_ref[0, g, :, i * wide : (i + 1) * wide].astype(F32),
            )
            out_ref[:, g * wide : (g + 1) * wide] = piece


def lay_rows(rep, here, there):
    _, groups, rows, wide = here.shape
    width = groups * wide // 4
    spec = pl.BlockSpec((1, groups, rows, wide), lambda j, rep_ref: (j // 2, 0, 0, 0))
    out = pl.BlockSpec((rows, width), lambda j, rep_ref: (rep_ref[0] ^ j, 0))
    return pl.pallas_call(
        lay_kernel,
        grid_spec=pltpu.PrefetchScalarGridSpec(
            num_scalar_prefetch=1, grid=(4,), in_specs=[spec, spec], out_specs=[out] * 4
        ),
        out_shape=[jax.ShapeDtypeStruct((4 * rows, width), F32)] * 4,
        cost_estimate=pl.CostEstimate(flops=0, bytes_accessed=here.size * 12, transcendentals=0),
    )(rep[None], here, there)


def cut_kernel(rep_ref, gate_ref, up_ref, down_ref, gate_out, up_out, down_out):
    del rep_ref
    gate_out[0] = gate_ref[...]
    up_out[0] = up_ref[...]
    down_out[0] = down_ref[...].T


def cut(rep, gate, up, down, groups, reps):
    rows, part = gate.shape[0], gate.shape[1] // (groups * reps)
    wide = pl.BlockSpec((rows, part), lambda g, rep_ref: (0, g * reps + rep_ref[0]))
    tall = pl.BlockSpec((part, rows), lambda g, rep_ref: (g * reps + rep_ref[0], 0))
    out = pl.BlockSpec((1, rows, part), lambda g, rep_ref: (g, 0, 0))
    return pl.pallas_call(
        cut_kernel,
        grid_spec=pltpu.PrefetchScalarGridSpec(
            num_scalar_prefetch=1, grid=(groups,), in_specs=[wide, wide, tall], out_specs=[out] * 3
        ),
        out_shape=[jax.ShapeDtypeStruct((groups, rows, part), BF)] * 3,
        cost_estimate=pl.CostEstimate(flops=0, bytes_accessed=groups * rows * part * 12, transcendentals=0),
    )(rep[None], gate, up, down)


def widen_kernel(x_ref, o_ref):
    for r in range(x_ref.shape[0]):
        wide = x_ref.shape[3]
        o_ref[:, r * wide : (r + 1) * wide] = x_ref[r, 0].astype(F32)


def widen_turned_kernel(x_ref, o_ref):
    for r in range(x_ref.shape[0]):
        tall = x_ref.shape[3]
        o_ref[r * tall : (r + 1) * tall, :] = x_ref[r, 0].astype(F32).T


def widen(parts, turned):
    reps, count, rows, wide = parts.shape
    out = (rows, reps * wide) if not turned else (reps * wide, rows)
    full = (rows, reps * count * wide) if not turned else (reps * count * wide, rows)
    return pl.pallas_call(
        widen_turned_kernel if turned else widen_kernel,
        grid=(count,),
        in_specs=[pl.BlockSpec((reps, 1, rows, wide), lambda s: (0, s, 0, 0))],
        out_specs=pl.BlockSpec(out, (lambda s: (s, 0)) if turned else (lambda s: (0, s))),
        out_shape=jax.ShapeDtypeStruct(full, F32),
        cost_estimate=pl.CostEstimate(flops=0, bytes_accessed=parts.size * 6, transcendentals=0),
    )(parts)


def put(buffer, part, starts):
    return lax.dynamic_update_slice(buffer, part, starts)


def rms(values, gains):
    return values * lax.rsqrt(jnp.mean(values * values, axis=-1, keepdims=True) + EPS) * gains


def angles_of(count):
    freqs = THETA ** (-2.0 * jnp.arange(HEAD // 2, dtype=F32) / HEAD)
    angles = jnp.arange(count, dtype=jnp.int32).astype(F32)[:, None] * freqs[None, :]
    return jnp.cos(angles), jnp.sin(angles)


def turn(values, cosine, sine):
    half = HEAD // 2
    out = []
    for start in range(0, values.shape[1], HEAD):
        first, second = values[:, start : start + half], values[:, start + half : start + HEAD]
        out += [first * cosine - second * sine, second * cosine + first * sine]
    return jnp.concatenate(out, axis=1)


def swiglu(gates, uppers):
    return jax.nn.silu(gates) * uppers


def attend(queries, keys, values):
    length = queries.shape[0]
    split = lambda a: a.reshape(length, -1, HEAD)
    scores = jnp.einsum("qhd,khd->hqk", split(queries), split(keys), preferred_element_type=F32)
    scores = scores * HEAD ** (-0.5)
    places = jnp.arange(length, dtype=jnp.int32)
    scores = jnp.where((places[None, :] <= places[:, None])[None], scores, -1e30)
    top = jnp.max(scores, axis=-1, keepdims=True)
    weights = jnp.exp(scores - top)
    totals = jnp.sum(weights, axis=-1, keepdims=True)
    probs = (weights / totals).astype(BF)
    mixed = jnp.einsum("hqk,khd->qhd", probs, split(values), preferred_element_type=F32)
    return mixed.reshape(length, -1).astype(BF), top + jnp.log(totals)


def attend_back(queries, keys, values, lse, grads):
    length = queries.shape[0]
    split = lambda a: a.reshape(length, -1, HEAD)
    scale = HEAD ** (-0.5)
    q, k, v, do = split(queries), split(keys), split(values), split(grads)
    scores = jnp.einsum("qhd,khd->hqk", q, k, preferred_element_type=F32) * scale
    places = jnp.arange(length, dtype=jnp.int32)
    scores = jnp.where((places[None, :] <= places[:, None])[None], scores, -1e30)
    probs = jnp.exp(scores - lse)
    d_probs = jnp.einsum("qhd,khd->hqk", do, v, preferred_element_type=F32)
    delta = jnp.sum(probs * d_probs, axis=-1, keepdims=True)
    ds = (probs * (d_probs - delta)).astype(BF)
    dv = jnp.einsum("hqk,qhd->khd", probs.astype(BF), do, preferred_element_type=F32)
    dq = jnp.einsum("hqk,khd->qhd", ds, k, preferred_element_type=F32) * scale
    dk = jnp.einsum("hqk,qhd->khd", ds, q, preferred_element_type=F32) * scale
    return dq.reshape(length, -1), dk.reshape(length, -1), dv.reshape(length, -1)


def by_heads(
    tokens, q_weight, k_weight, v_weight, o_weight, gate_weight, up_weight, down_weight,
    q_gain, k_gain, attn_gain, mlp_gain, cotangent,
):
    x = tokens[0]
    count, width = x.shape
    groups = lax.axis_size("grp")
    reps = 4
    me, rep = lax.axis_index("grp"), lax.axis_index("rep")
    length = count * groups
    own = width // groups
    hidden = gate_weight.shape[1]
    block = hidden // groups
    part = block // reps
    sub = own // reps
    zero = jnp.int32(0)
    at = [me ^ k for k in range(groups)]
    of = [rep ^ j for j in range(reps)]

    qkv_rows = jnp.concatenate(
        [
            lax.dynamic_slice(w, (rep * sub, zero), (sub, width)).reshape(sub, groups, own)
            for w in (q_weight, k_weight, v_weight)
        ],
        axis=2,
    )
    gains = jnp.pad(jnp.concatenate([attn_gain, mlp_gain])[None], ((0, 7), (0, own)))
    gains = jnp.broadcast_to(gains[None], (groups, 8, 3 * own))
    landed = to_columns(jnp.concatenate([jnp.transpose(qkv_rows, (1, 0, 2)), gains], axis=1))
    gain_all = landed[:, sub, : 2 * own].astype(F32).reshape(groups, 2, own)
    ga, gm = gain_all[:, 0].reshape(width), gain_all[:, 1].reshape(width)
    mine = landed[:, :sub]
    far = rep_far(mine)
    x_pieces = gather_pieces(x, far)
    near = rep_near(jnp.stack([mine, far]))
    w_qkv = jnp.zeros((groups, reps, sub, 3 * own), BF)
    for j, piece in enumerate([mine, near[0], far, near[1]]):
        w_qkv = put(w_qkv, piece[:, None], (zero, of[j], zero, zero))
    w_qkv = w_qkv.reshape(width, 3 * own)

    x_all = jnp.zeros((groups, count, width), BF)
    for k, piece in enumerate(x_pieces):
        x_all = put(x_all, piece[None], (at[k], zero, zero))
    x_all = x_all.reshape(length, width)

    sends = cut(rep, gate_weight, up_weight, down_weight, groups, reps)

    def spread(blocks):
        return lax.all_gather(blocks.reshape(width, part), "rep", axis=1, tiled=True)

    gq, gk = q_gain.astype(F32), k_gain.astype(F32)
    cosine, sine = angles_of(length)
    qkv = dot(x_all, w_qkv)
    q_proj, k_proj = qkv[:, :own], qkv[:, own : 2 * own]
    values = qkv[:, 2 * own :].astype(BF)
    squares = jnp.stack([jnp.sum(q_proj * q_proj, axis=1), jnp.sum(k_proj * k_proj, axis=1)])
    squares = group_sum(squares)
    q_inv = lax.rsqrt(squares[0] / width + EPS)[:, None]
    k_inv = lax.rsqrt(squares[1] / width + EPS)[:, None]
    queries = turn(q_proj * q_inv * gq, cosine, sine).astype(BF)
    keys = turn(k_proj * k_inv * gk, cosine, sine).astype(BF)
    attn, lse = attend(queries, keys, values)
    gu_landed = tie(to_columns(tie(jnp.concatenate(sends[:2], axis=2), x_all)), attn)
    w_gate, w_up = spread(gu_landed[..., :part]), spread(gu_landed[..., part:])
    a_part = dot(attn, o_weight)
    a_proj, _ = scatter_sum(
        [lax.dynamic_slice(a_part, (at[k] * count, zero), (count, width)) for k in range(groups)]
    )
    w_down = spread(tie(to_columns(tie(sends[2], attn)), a_proj))
    middle = x.astype(F32) + rms(a_proj, ga)
    middle_bf = middle.astype(BF)

    def halves(pieces):
        return jnp.concatenate(pieces[0::2]), jnp.concatenate(pieces[1::2])

    def whole(even, odd):
        even, odd = (v.reshape(groups // 2, count, width) for v in (even, odd))
        return [(even, odd)[k % 2][k // 2] for k in range(groups)]

    h_halves = halves(gather_pieces(middle_bf, w_gate))
    gates = [dot(h, w_gate) for h in h_halves]
    uppers = [dot(h, w_up) for h in h_halves]
    mixed = [swiglu(g, u).astype(BF) for g, u in zip(gates, uppers)]
    y_proj, _ = scatter_sum(whole(*[dot_right_t(m, w_down) for m in mixed]))
    outputs = (middle + rms(y_proj, gm)).astype(BF)

    grad_out = cotangent[0].astype(F32)
    _, pull = jax.vjp(rms, y_proj, gm)
    dy, d_mlp_gain = pull(grad_out)
    dy_halves = halves(gather_pieces(dy.astype(BF)))
    d_gates, d_uppers, m_halves = [], [], []
    for g, u, d in zip(gates, uppers, dy_halves):
        _, pull = jax.vjp(swiglu, g, u)
        d_gate, d_upper = (v.astype(BF) for v in pull(dot(d, w_down)))
        d_gates.append(d_gate)
        d_uppers.append(d_upper)
        m_halves.append(dot_right_t(d_gate, w_gate) + dot_right_t(d_upper, w_up))
    d_middle, _ = scatter_sum(whole(*m_halves))
    d_middle = grad_out + d_middle

    def weight_sum(left, right, later):
        both = [dot_left_t(a, b) for a, b in zip(left, right)]
        both = tie((both[0] + both[1]).astype(BF), later)
        return lax.psum_scatter(both, "rep", scatter_dimension=1, tiled=True)

    def to_place(sums, before, after):
        return tie(to_columns(tie(sums.reshape(groups, own, part), before)), after)

    def to_rows(sums, turned):
        return widen(lax.all_gather(lax.optimization_barrier(sums), "rep", axis=0), turned)

    _, pull = jax.vjp(rms, a_proj, ga)
    da, d_attn_gain = pull(d_middle)
    da_bf = da.astype(BF)
    sum_down = weight_sum(dy_halves, mixed, da_bf)
    sum_gate = weight_sum(h_halves, d_gates, da_bf)
    sum_up = weight_sum(h_halves, d_uppers, da_bf)
    da_pieces = gather_pieces(da_bf)
    da_all = jnp.zeros((groups, count, width), BF)
    for k, piece in enumerate(da_pieces):
        da_all = put(da_all, piece[None], (at[k], zero, zero))
    da_all = da_all.reshape(length, width)
    d_attn = dot_right_t(da_all, o_weight).astype(BF)
    dq, dk, dv = attend_back(queries, keys, values, lse, d_attn)
    down_grad = to_rows(to_place(sum_down, da_all, dq), True)
    dq, dk = turn(dq, cosine, -sine), turn(dk, cosine, -sine)
    q_unit, k_unit = q_proj * q_inv, k_proj * k_inv
    d_q_gain, d_k_gain = jnp.sum(dq * q_unit, axis=0), jnp.sum(dk * k_unit, axis=0)
    dq, dk = dq * gq, dk * gk
    along = jnp.concatenate(
        [jnp.sum(dq * q_unit, axis=1), jnp.sum(dk * k_unit, axis=1), d_attn_gain, d_mlp_gain]
    )
    along = group_sum(along.reshape(-1, 128)).reshape(-1)
    q_mean, k_mean = along[:length, None] / width, along[length : 2 * length, None] / width
    d_qkv = jnp.concatenate(
        [
            (q_inv * (dq - q_unit * q_mean)).astype(BF),
            (k_inv * (dk - k_unit * k_mean)).astype(BF),
            dv.astype(BF),
        ],
        axis=1,
    )
    x_part = dot_right_t(d_qkv, w_qkv)
    gate_grad = to_rows(to_place(sum_gate, along, x_part), False)

    g_qkv = dot_left_t(x_all, d_qkv).astype(BF).reshape(groups, reps, sub, 3 * own)
    g_o = dot_left_t(attn, tie(da_all, dq)).astype(BF).reshape(reps, sub, groups, own)
    g_all = jnp.concatenate([g_qkv, jnp.transpose(g_o, (2, 0, 1, 3))], axis=3)
    parts = [
        lax.dynamic_slice(g_all, (zero, of[j], zero, zero), (groups, 1, sub, 4 * own))[:, 0] for j in range(reps)
    ]
    near = near_send(parts)
    far = far_send(parts, near)
    d_x, _ = scatter_sum(
        [lax.dynamic_slice(x_part, (at[k] * count, zero), (count, width)) for k in range(groups)], far
    )
    up_grad = to_rows(to_place(sum_up, x_part, d_x), False)
    sums = rep_total(parts, near, far)
    rows_of = tie(to_columns(sums[..., : 3 * own]), d_x)
    d_x = d_middle + tie(d_x, down_grad)
    mine = jnp.concatenate([rows_of, sums[..., 3 * own :]], axis=2)
    mine = tie(mine, down_grad)
    far = rep_far(mine)
    here = tie(jnp.stack([mine, far]), gate_grad)
    q_grad, k_grad, v_grad, o_grad = lay_rows(rep, here, rep_near(here))

    post = lax.dynamic_slice(along[2 * length :].reshape(2, width), (zero, me * own), (2, own))
    gain_sums = jnp.concatenate([jnp.stack([d_q_gain, d_k_gain]), post])
    for step in (1, 2):
        gain_sums = gain_sums + shuffle(gain_sums, "rep", step)
    return (
        outputs[None], d_x.astype(BF)[None], q_grad, k_grad, v_grad, o_grad, gate_grad, up_grad, down_grad,
        gain_sums[0], gain_sums[1], gain_sums[2], gain_sums[3],
    )


def rotary(values, places):
    count = values.shape[0]
    heads = values.reshape(count, HEADS, HEAD)
    freqs = THETA ** (-2.0 * jnp.arange(HEAD // 2, dtype=jnp.float32) / HEAD)
    angles = places[:, None] * freqs[None, :]
    cosine = jnp.cos(angles)[:, None, :]
    sine = jnp.sin(angles)[:, None, :]
    first = heads[..., : HEAD // 2]
    second = heads[..., HEAD // 2 :]
    turned = jnp.concatenate(
        [first * cosine - second * sine, second * cosine + first * sine], axis=-1
    )
    return turned.reshape(count, HEADS * HEAD)


def head_slice(matrix, index):
    piece = lax.dynamic_slice_in_dim(matrix, index * GROUPED * HEAD, GROUPED * HEAD, 1)
    return piece.reshape(matrix.shape[0], GROUPED, HEAD)


def heads_back(stacked, count):
    return jnp.moveaxis(stacked, 0, 1).reshape(count, HEADS * HEAD)


def by_tokens(
    tokens,
    q_weight,
    k_weight,
    v_weight,
    o_weight,
    gate_weight,
    up_weight,
    down_weight,
    q_gain,
    k_gain,
    attn_gain,
    mlp_gain,
    cotangent,
):
    inputs = tokens[0]
    rows = inputs.shape[0]
    width = inputs.shape[1]
    groups = lax.axis_size("grp")
    length = rows * groups
    query_places = lax.axis_index("grp") * rows + jnp.arange(rows, dtype=jnp.int32)
    places = query_places.astype(jnp.float32)
    scale = HEAD ** (-0.5)
    group_ids = jnp.arange(HEADS // GROUPED, dtype=jnp.int32)
    wq_fwd, wk_fwd, wv_fwd, wo_gathered, gq_bf, gk_bf, ga_bf = (
        lax.all_gather(q_weight, "grp", axis=0, tiled=True),
        lax.all_gather(k_weight, "grp", axis=0, tiled=True),
        lax.all_gather(v_weight, "grp", axis=0, tiled=True),
        lax.all_gather(o_weight, "grp", axis=0, tiled=True),
        lax.all_gather(q_gain, "grp", axis=0, tiled=True),
        lax.all_gather(k_gain, "grp", axis=0, tiled=True),
        lax.all_gather(attn_gain, "grp", axis=0, tiled=True),
    )
    gq_full = gq_bf.astype(jnp.float32)
    gk_full = gk_bf.astype(jnp.float32)
    ga_full = ga_bf.astype(jnp.float32)
    q_proj = dot(inputs, wq_fwd)
    k_proj = dot(inputs, wk_fwd)
    v_proj = dot(inputs, wv_fwd)

    def turn_query(values, gains):
        return rotary(rms(values, gains), places)

    queries = turn_query(q_proj, gq_full).astype(jnp.bfloat16)
    keys_own = turn_query(k_proj, gk_full).astype(jnp.bfloat16)
    values_own = v_proj.astype(jnp.bfloat16)
    keys_all, values_all = (
        lax.all_gather(keys_own, "grp", axis=0, tiled=True),
        lax.all_gather(values_own, "grp", axis=0, tiled=True),
    )
    allowed = jnp.arange(length, dtype=jnp.int32)[None, :] <= query_places[:, None]

    def forward_group(index):
        scores = (
            jnp.einsum(
                "qhd,khd->hqk",
                head_slice(queries, index),
                head_slice(keys_all, index),
                preferred_element_type=jnp.float32,
            )
            * scale
        )
        scores = jnp.where(allowed[None], scores, -1e30)
        top_score = jnp.max(scores, axis=-1, keepdims=True)
        weights = jnp.exp(scores - top_score)
        totals = jnp.sum(weights, axis=-1, keepdims=True)
        probs = (weights / totals).astype(jnp.bfloat16)
        mixed = jnp.einsum(
            "hqk,khd->qhd", probs, head_slice(values_all, index), preferred_element_type=jnp.float32
        )
        return (mixed, (top_score + jnp.log(totals))[..., 0])

    mixed_all, log_totals = lax.map(forward_group, group_ids)
    log_totals = log_totals.reshape(HEADS, rows)
    attn_bf = heads_back(mixed_all, rows).astype(jnp.bfloat16)
    a_proj = dot(attn_bf, wo_gathered)
    middle = inputs.astype(jnp.float32) + rms(a_proj, ga_full)
    middle_bf = middle.astype(jnp.bfloat16)
    wg_fwd, wu_fwd, gm_bf = (
        lax.all_gather(gate_weight, "grp", axis=0, tiled=True),
        lax.all_gather(up_weight, "grp", axis=0, tiled=True),
        lax.all_gather(mlp_gain, "grp", axis=0, tiled=True),
    )
    gm_full = gm_bf.astype(jnp.float32)
    gates = dot(middle_bf, wg_fwd)
    uppers = dot(middle_bf, wu_fwd)
    hidden = swiglu(gates, uppers).astype(jnp.bfloat16)
    y_proj = dot(hidden, lax.all_gather(down_weight, "grp", axis=1, tiled=True))
    outputs = (middle + rms(y_proj, gm_full)).astype(jnp.bfloat16)
    grad_out = cotangent[0].astype(jnp.float32)
    unused_y, pull_mlp = jax.vjp(rms, y_proj, gm_full)
    dy_proj, d_mlp_gain = pull_mlp(grad_out)
    dy_bf = dy_proj.astype(jnp.bfloat16)
    down_full = lax.all_gather(down_weight, "grp", axis=1, tiled=True)
    d_hidden = dot_right_t(dy_bf, down_full)
    unused_h, pull_act = jax.vjp(swiglu, gates, uppers)
    d_gates, d_uppers = pull_act(d_hidden)
    dg_bf = d_gates.astype(jnp.bfloat16)
    du_bf = d_uppers.astype(jnp.bfloat16)
    block = dot_right_t(
        dg_bf, lax.all_gather(gate_weight, "grp", axis=0, tiled=True)
    ) + dot_right_t(du_bf, lax.all_gather(up_weight, "grp", axis=0, tiled=True))
    d_middle = grad_out + block
    unused_a, pull_attn = jax.vjp(rms, a_proj, ga_full)
    da_proj, d_attn_gain = pull_attn(d_middle)
    da_bf = da_proj.astype(jnp.bfloat16)
    wq_full, wk_full, wv_full, wo_full = (
        lax.all_gather(q_weight, "grp", axis=0, tiled=True),
        lax.all_gather(k_weight, "grp", axis=0, tiled=True),
        lax.all_gather(v_weight, "grp", axis=0, tiled=True),
        lax.all_gather(o_weight, "grp", axis=0, tiled=True),
    )
    d_attn_bf = dot_right_t(da_bf, wo_full).astype(jnp.bfloat16)

    def query_group(index):
        query_g = head_slice(queries, index)
        key_g = head_slice(keys_all, index)
        dout_g = head_slice(d_attn_bf, index)
        lse_g = lax.dynamic_slice_in_dim(log_totals, index * GROUPED, GROUPED, 0)
        scores = (
            jnp.einsum("qhd,khd->hqk", query_g, key_g, preferred_element_type=jnp.float32) * scale
        )
        scores = jnp.where(allowed[None], scores, -1e30)
        probs = jnp.exp(scores - lse_g[..., None])
        d_probs = jnp.einsum(
            "qhd,khd->hqk",
            dout_g,
            head_slice(values_all, index),
            preferred_element_type=jnp.float32,
        )
        deltas = jnp.sum(probs * d_probs, axis=-1, keepdims=True)
        ds_bf = (probs * (d_probs - deltas)).astype(jnp.bfloat16)
        d_query = (
            jnp.einsum("hqk,khd->qhd", ds_bf, key_g, preferred_element_type=jnp.float32) * scale
        )
        return (d_query, deltas[..., 0])

    d_query_all, delta_all = lax.map(query_group, group_ids)
    d_queries = heads_back(d_query_all, rows)
    delta_all = delta_all.reshape(HEADS, rows)
    key_places = jnp.arange(rows * lax.axis_size("grp"), dtype=jnp.int32)
    permit = key_places[None, :] <= query_places[:, None]

    def key_group(index):
        query_g = head_slice(queries, index)
        dout_g = head_slice(d_attn_bf, index)
        lse_g = lax.dynamic_slice_in_dim(log_totals, index * GROUPED, GROUPED, 0)
        delta_g = lax.dynamic_slice_in_dim(delta_all, index * GROUPED, GROUPED, 0)
        scores = (
            jnp.einsum(
                "qhd,khd->hqk",
                query_g,
                head_slice(keys_all, index),
                preferred_element_type=jnp.float32,
            )
            * scale
        )
        scores = jnp.where(permit[None], scores, -1e30)
        probs = jnp.exp(scores - lse_g[..., None])
        d_value = jnp.einsum(
            "hqk,qhd->khd", probs.astype(jnp.bfloat16), dout_g, preferred_element_type=jnp.float32
        )
        d_probs = jnp.einsum(
            "qhd,khd->hqk",
            dout_g,
            head_slice(values_all, index),
            preferred_element_type=jnp.float32,
        )
        ds_bf = (probs * (d_probs - delta_g[..., None])).astype(jnp.bfloat16)
        d_key = (
            jnp.einsum("hqk,qhd->khd", ds_bf, query_g, preferred_element_type=jnp.float32) * scale
        )
        return (d_key, d_value)

    d_key_all, d_value_all = lax.map(key_group, group_ids)
    key_grads = lax.psum_scatter(
        jnp.concatenate(
            [
                heads_back(d_key_all, rows * lax.axis_size("grp")),
                heads_back(d_value_all, rows * lax.axis_size("grp")),
            ],
            axis=1,
        ),
        "grp",
        scatter_dimension=0,
        tiled=True,
    )
    dv_bf = key_grads[:, width:].astype(jnp.bfloat16)
    unused_q, pull_query = jax.vjp(turn_query, q_proj, gq_full)
    dq_proj, d_q_gain = pull_query(d_queries)
    unused_k, pull_key = jax.vjp(turn_query, k_proj, gk_full)
    dk_proj, d_k_gain = pull_key(key_grads[:, :width])
    dq_bf = dq_proj.astype(jnp.bfloat16)
    dk_bf = dk_proj.astype(jnp.bfloat16)
    d_inputs = (
        d_middle
        + dot_right_t(dq_bf, wq_full)
        + dot_right_t(dk_bf, wk_full)
        + dot_right_t(dv_bf, wv_full)
    )
    owned_rows = width // groups
    pairs = (
        (inputs, dq_bf), (inputs, dk_bf), (inputs, dv_bf), (attn_bf, da_bf),
        (middle_bf, dg_bf), (middle_bf, du_bf), (dy_bf, hidden),
    )
    weight_sums = []
    for left, right in pairs:
        if weight_sums:
            left, right, weight_sums[-1] = lax.optimization_barrier((left, right, weight_sums[-1]))
        share = lax.psum_scatter(dot_left_t(left, right), "grp", scatter_dimension=0, tiled=True)
        weight_sums.append(lax.psum(share, "rep"))
    gain_stack = jnp.stack([d_q_gain, d_k_gain, d_attn_gain, d_mlp_gain])
    gain_total = lax.psum(gain_stack, ("rep", "grp"))
    gain_mine = lax.dynamic_slice_in_dim(
        gain_total, lax.axis_index("grp") * owned_rows, owned_rows, 1
    )
    return (
        outputs[None],
        d_inputs.astype(jnp.bfloat16)[None],
        *weight_sums[:6],
        weight_sums[6].T,
        gain_mine[0],
        gain_mine[1],
        gain_mine[2],
        gain_mine[3],
    )


def solution(mesh):
    rows = P("grp", None)
    seq = P("rep", "grp", None)
    gain = P("grp")
    whole_heads = HEADS % mesh.shape["grp"] == 0 and mesh.shape["rep"] == 4
    return jax.shard_map(
        by_heads if whole_heads else by_tokens,
        mesh=mesh,
        in_specs=(seq, *[rows] * 6, P(None, "grp"), *[gain] * 4, seq),
        out_specs=(seq, seq, *[rows] * 6, P(None, "grp"), *[gain] * 4),
        check_vma=False,
    )
```

```python
import jax
import jax.numpy as jnp
from jax import lax
from jax.experimental import pallas as pl
from jax.experimental.pallas import tpu as pltpu
from jax.sharding import PartitionSpec as P

HEADS = 16
HEAD = 128
EPS = 1e-06
THETA = 500000.0
GROUPED = 4
BF = jnp.bfloat16
F32 = jnp.float32


def dot(left, right, dims=((1,), (0,)), kind=F32):
    return lax.dot_general(left, right, (dims, ((), ())), preferred_element_type=kind)


def dot_right_t(left, right):
    return dot(left, right, ((1,), (1,)))


def dot_left_t(left, right):
    return dot(left, right, ((0,), (0,)))


def shuffle(value, axis, step):
    return lax.ppermute(value, axis, [(i, i ^ step) for i in range(lax.axis_size(axis))])


def tie(value, *others):
    return lax.optimization_barrier((value, *others))[0]


def gather_pieces(value, *meanwhile):
    count = lax.axis_size("grp")
    top = count - 2
    pieces = [None] * count
    pieces[0] = value
    pieces[top] = shuffle(value, "grp", top)
    for step in range(2, count // 2, 2):
        pieces[step] = shuffle(value, "grp", step)
    pieces[1] = shuffle(value, "grp", 1)
    for step in range(count // 2, top, 2):
        pieces[step] = shuffle(pieces[top], "grp", step ^ top)
    steps = [*range(2, count // 2, 2), top, *range(count // 2, top, 2)]
    for step in steps:
        held = meanwhile if step == steps[-1] else ()
        pieces[step + 1] = shuffle(tie(pieces[step], *held) if held else pieces[step], "grp", 1)
    return pieces


def scatter_sum(pieces, *meanwhile):
    count = len(pieces)
    top = count - 2
    odd = {k: shuffle(pieces[k + 1].astype(BF), "grp", 1) for k in range(count // 2, top, 2)}
    odd |= {k: shuffle(pieces[k + 1].astype(BF), "grp", 1) for k in (top, *range(2, count // 2, 2), 0)}
    paired = {k: pieces[k].astype(F32) + odd[k].astype(F32) for k in range(count // 2, top, 2)}
    passed = [shuffle(v.astype(BF), "grp", k ^ top) for k, v in paired.items()]
    held = tie(odd[top], *passed) if passed else odd[top]
    farthest = pieces[top].astype(F32) + held.astype(F32) + sum(v.astype(F32) for v in passed)
    farthest = shuffle(farthest.astype(BF), "grp", top)
    total = pieces[0].astype(F32)
    last = []
    for k in range(2, count // 2, 2):
        held = tie(odd[k], *passed, *meanwhile)
        last.append(shuffle((pieces[k].astype(F32) + held.astype(F32)).astype(BF), "grp", k))
        total += last[-1].astype(F32)
    return total + farthest.astype(F32) + odd[0].astype(F32), last


def to_columns(blocks):
    return lax.all_to_all(blocks, "grp", 0, 0, tiled=True)


def group_sum(value):
    step = 1
    while step < lax.axis_size("grp"):
        value = value + shuffle(value, "grp", step)
        step *= 2
    return value


def rep_near(value):
    return shuffle(value, "rep", 1)


def rep_far(value):
    return shuffle(value, "rep", 2)


def near_send(parts):
    return rep_near(jnp.stack([parts[1], parts[3]]))


def far_send(parts, near):
    return rep_far((parts[2].astype(F32) + near[1].astype(F32)).astype(BF))


def rep_total(parts, near, far):
    return (parts[0].astype(F32) + near[0].astype(F32) + far.astype(F32)).astype(BF)


def lay_kernel(rep_ref, here_ref, there_ref, *out_refs):
    del rep_ref
    wide = here_ref.shape[3] // len(out_refs)
    here = pl.program_id(0) % 2 == 0
    for i, out_ref in enumerate(out_refs):
        for g in range(here_ref.shape[1]):
            piece = jnp.where(
                here,
                here_ref[0, g, :, i * wide : (i + 1) * wide].astype(F32),
                there_ref[0, g, :, i * wide : (i + 1) * wide].astype(F32),
            )
            out_ref[:, g * wide : (g + 1) * wide] = piece


def lay_rows(rep, here, there):
    _, groups, rows, wide = here.shape
    width = groups * wide // 4
    spec = pl.BlockSpec((1, groups, rows, wide), lambda j, rep_ref: (j // 2, 0, 0, 0))
    out = pl.BlockSpec((rows, width), lambda j, rep_ref: (rep_ref[0] ^ j, 0))
    return pl.pallas_call(
        lay_kernel,
        grid_spec=pltpu.PrefetchScalarGridSpec(
            num_scalar_prefetch=1, grid=(4,), in_specs=[spec, spec], out_specs=[out] * 4
        ),
        out_shape=[jax.ShapeDtypeStruct((4 * rows, width), F32)] * 4,
        cost_estimate=pl.CostEstimate(flops=0, bytes_accessed=here.size * 12, transcendentals=0),
    )(rep[None], here, there)


def cut_kernel(rep_ref, gate_ref, up_ref, down_ref, gate_out, up_out, down_out):
    del rep_ref
    gate_out[0] = gate_ref[...]
    up_out[0] = up_ref[...]
    down_out[0] = down_ref[...].T


def cut(rep, gate, up, down, groups, reps):
    rows, part = gate.shape[0], gate.shape[1] // (groups * reps)
    wide = pl.BlockSpec((rows, part), lambda g, rep_ref: (0, g * reps + rep_ref[0]))
    tall = pl.BlockSpec((part, rows), lambda g, rep_ref: (g * reps + rep_ref[0], 0))
    out = pl.BlockSpec((1, rows, part), lambda g, rep_ref: (g, 0, 0))
    return pl.pallas_call(
        cut_kernel,
        grid_spec=pltpu.PrefetchScalarGridSpec(
            num_scalar_prefetch=1, grid=(groups,), in_specs=[wide, wide, tall], out_specs=[out] * 3
        ),
        out_shape=[jax.ShapeDtypeStruct((groups, rows, part), BF)] * 3,
        cost_estimate=pl.CostEstimate(flops=0, bytes_accessed=groups * rows * part * 12, transcendentals=0),
    )(rep[None], gate, up, down)


def widen_kernel(x_ref, o_ref):
    for r in range(x_ref.shape[0]):
        wide = x_ref.shape[3]
        o_ref[:, r * wide : (r + 1) * wide] = x_ref[r, 0].astype(F32)


def widen_turned_kernel(x_ref, o_ref):
    for r in range(x_ref.shape[0]):
        tall = x_ref.shape[3]
        o_ref[r * tall : (r + 1) * tall, :] = x_ref[r, 0].astype(F32).T


def widen(parts, turned):
    reps, count, rows, wide = parts.shape
    out = (rows, reps * wide) if not turned else (reps * wide, rows)
    full = (rows, reps * count * wide) if not turned else (reps * count * wide, rows)
    return pl.pallas_call(
        widen_turned_kernel if turned else widen_kernel,
        grid=(count,),
        in_specs=[pl.BlockSpec((reps, 1, rows, wide), lambda s: (0, s, 0, 0))],
        out_specs=pl.BlockSpec(out, (lambda s: (s, 0)) if turned else (lambda s: (0, s))),
        out_shape=jax.ShapeDtypeStruct(full, F32),
        cost_estimate=pl.CostEstimate(flops=0, bytes_accessed=parts.size * 6, transcendentals=0),
    )(parts)


def put(buffer, part, starts):
    return lax.dynamic_update_slice(buffer, part, starts)


def rms(values, gains):
    return values * lax.rsqrt(jnp.mean(values * values, axis=-1, keepdims=True) + EPS) * gains


def angles_of(count):
    freqs = THETA ** (-2.0 * jnp.arange(HEAD // 2, dtype=F32) / HEAD)
    angles = jnp.arange(count, dtype=jnp.int32).astype(F32)[:, None] * freqs[None, :]
    return jnp.cos(angles), jnp.sin(angles)


def turn(values, cosine, sine):
    half = HEAD // 2
    out = []
    for start in range(0, values.shape[1], HEAD):
        first, second = values[:, start : start + half], values[:, start + half : start + HEAD]
        out += [first * cosine - second * sine, second * cosine + first * sine]
    return jnp.concatenate(out, axis=1)


def swiglu(gates, uppers):
    return jax.nn.silu(gates) * uppers


def attend(queries, keys, values):
    length = queries.shape[0]
    split = lambda a: a.reshape(length, -1, HEAD)
    scores = jnp.einsum("qhd,khd->hqk", split(queries), split(keys), preferred_element_type=F32)
    scores = scores * HEAD ** (-0.5)
    places = jnp.arange(length, dtype=jnp.int32)
    scores = jnp.where((places[None, :] <= places[:, None])[None], scores, -1e30)
    top = jnp.max(scores, axis=-1, keepdims=True)
    weights = jnp.exp(scores - top)
    totals = jnp.sum(weights, axis=-1, keepdims=True)
    probs = (weights / totals).astype(BF)
    mixed = jnp.einsum("hqk,khd->qhd", probs, split(values), preferred_element_type=F32)
    return mixed.reshape(length, -1).astype(BF), top + jnp.log(totals)


def attend_back(queries, keys, values, lse, grads):
    length = queries.shape[0]
    split = lambda a: a.reshape(length, -1, HEAD)
    scale = HEAD ** (-0.5)
    q, k, v, do = split(queries), split(keys), split(values), split(grads)
    scores = jnp.einsum("qhd,khd->hqk", q, k, preferred_element_type=F32) * scale
    places = jnp.arange(length, dtype=jnp.int32)
    scores = jnp.where((places[None, :] <= places[:, None])[None], scores, -1e30)
    probs = jnp.exp(scores - lse)
    d_probs = jnp.einsum("qhd,khd->hqk", do, v, preferred_element_type=F32)
    delta = jnp.sum(probs * d_probs, axis=-1, keepdims=True)
    ds = (probs * (d_probs - delta)).astype(BF)
    dv = jnp.einsum("hqk,qhd->khd", probs.astype(BF), do, preferred_element_type=F32)
    dq = jnp.einsum("hqk,khd->qhd", ds, k, preferred_element_type=F32) * scale
    dk = jnp.einsum("hqk,qhd->khd", ds, q, preferred_element_type=F32) * scale
    return dq.reshape(length, -1), dk.reshape(length, -1), dv.reshape(length, -1)


def by_heads(
    tokens, q_weight, k_weight, v_weight, o_weight, gate_weight, up_weight, down_weight,
    q_gain, k_gain, attn_gain, mlp_gain, cotangent,
):
    x = tokens[0]
    count, width = x.shape
    groups = lax.axis_size("grp")
    reps = 4
    me, rep = lax.axis_index("grp"), lax.axis_index("rep")
    length = count * groups
    own = width // groups
    hidden = gate_weight.shape[1]
    block = hidden // groups
    part = block // reps
    sub = own // reps
    zero = jnp.int32(0)
    at = [me ^ k for k in range(groups)]
    of = [rep ^ j for j in range(reps)]

    qkv_rows = jnp.concatenate(
        [
            lax.dynamic_slice(w, (rep * sub, zero), (sub, width)).reshape(sub, groups, own)
            for w in (q_weight, k_weight, v_weight)
        ],
        axis=2,
    )
    gains = jnp.pad(jnp.concatenate([attn_gain, mlp_gain])[None], ((0, 7), (0, own)))
    gains = jnp.broadcast_to(gains[None], (groups, 8, 3 * own))
    landed = to_columns(jnp.concatenate([jnp.transpose(qkv_rows, (1, 0, 2)), gains], axis=1))
    gain_all = landed[:, sub, : 2 * own].astype(F32).reshape(groups, 2, own)
    ga, gm = gain_all[:, 0].reshape(width), gain_all[:, 1].reshape(width)
    mine = landed[:, :sub]
    far = rep_far(mine)
    x_pieces = gather_pieces(x)
    near = rep_near(jnp.stack([mine, far]))
    w_qkv = jnp.zeros((groups, reps, sub, 3 * own), BF)
    for j, piece in enumerate([mine, near[0], far, near[1]]):
        w_qkv = put(w_qkv, piece[:, None], (zero, of[j], zero, zero))
    w_qkv = w_qkv.reshape(width, 3 * own)

    x_all = jnp.zeros((groups, count, width), BF)
    for k, piece in enumerate(x_pieces):
        x_all = put(x_all, piece[None], (at[k], zero, zero))
    x_all = x_all.reshape(length, width)

    sends = cut(rep, gate_weight, up_weight, down_weight, groups, reps)

    def spread(blocks):
        return lax.all_gather(blocks.reshape(width, part), "rep", axis=1, tiled=True)

    gq, gk = q_gain.astype(F32), k_gain.astype(F32)
    cosine, sine = angles_of(length)
    qkv = dot(x_all, w_qkv)
    q_proj, k_proj = qkv[:, :own], qkv[:, own : 2 * own]
    values = qkv[:, 2 * own :].astype(BF)
    squares = jnp.stack([jnp.sum(q_proj * q_proj, axis=1), jnp.sum(k_proj * k_proj, axis=1)])
    squares = group_sum(squares)
    q_inv = lax.rsqrt(squares[0] / width + EPS)[:, None]
    k_inv = lax.rsqrt(squares[1] / width + EPS)[:, None]
    queries = turn(q_proj * q_inv * gq, cosine, sine).astype(BF)
    keys = turn(k_proj * k_inv * gk, cosine, sine).astype(BF)
    attn, lse = attend(queries, keys, values)
    gu_landed = tie(to_columns(tie(jnp.concatenate(sends[:2], axis=2), x_pieces[groups - 1])), squares)
    w_gate, w_up = spread(gu_landed[..., :part]), spread(gu_landed[..., part:])
    a_part = dot(attn, o_weight).astype(BF)
    a_proj, _ = scatter_sum(
        [lax.dynamic_slice(a_part, (at[k] * count, zero), (count, width)) for k in range(groups)]
    )
    w_down = spread(tie(to_columns(tie(sends[2], gu_landed)), attn))
    middle = x.astype(F32) + rms(a_proj, ga)
    middle_bf = middle.astype(BF)

    def halves(pieces):
        return jnp.concatenate(pieces[0::2]), jnp.concatenate(pieces[1::2])

    def whole(*parts):
        parts = [v.reshape(-1, count, width) for v in parts]
        return [parts[k % len(parts)][k // len(parts)] for k in range(groups)]

    h_halves = halves(gather_pieces(middle_bf, w_gate))
    gates = [dot(h, w_gate) for h in h_halves]
    uppers = [dot(h, w_up) for h in h_halves]
    mixed = [swiglu(g, u).astype(BF) for g, u in zip(gates, uppers)]
    y_proj, _ = scatter_sum(whole(*[dot_right_t(m, w_down).astype(BF) for m in mixed]))
    outputs = (middle + rms(y_proj, gm)).astype(BF)

    grad_out = cotangent[0].astype(F32)
    _, pull = jax.vjp(rms, y_proj, gm)
    dy, d_mlp_gain = pull(grad_out)
    dy_pieces = gather_pieces(dy.astype(BF))
    dy_halves = halves([tie(dy_pieces[0], dy_pieces[groups - 1]), *dy_pieces[1:]])
    d_gates, d_uppers, m_halves = [], [], []
    for g, u, d in zip(gates, uppers, dy_halves):
        _, pull = jax.vjp(swiglu, g, u)
        d_gate, d_upper = (v.astype(BF) for v in pull(dot(d, w_down)))
        d_gates.append(d_gate)
        d_uppers.append(d_upper)
        m_halves.append((dot_right_t(d_gate, w_gate) + dot_right_t(d_upper, w_up)).astype(BF))
    d_middle, _ = scatter_sum(whole(*m_halves))
    d_middle = grad_out + d_middle

    def weight_part(left, right):
        return sum(dot_left_t(a, b) for a, b in zip(left, right)).astype(BF)

    def over_rep(part_sum):
        return lax.psum_scatter(part_sum, "rep", scatter_dimension=1, tiled=True)

    def to_place(sums, before, after):
        return tie(to_columns(tie(sums.reshape(groups, own, part), before)), after)

    def to_rows(sums, turned):
        return widen(lax.all_gather(lax.optimization_barrier(sums), "rep", axis=0), turned)

    g_down = weight_part(dy_halves, mixed)
    g_gate, g_up = weight_part(h_halves, d_gates), weight_part(h_halves, d_uppers)
    sum_down = over_rep(tie(g_down, *m_halves))
    d_middle = tie(d_middle, sum_down, g_gate, g_up)
    _, pull = jax.vjp(rms, a_proj, ga)
    da, d_attn_gain = pull(d_middle)
    da_bf = da.astype(BF)
    sum_gate, sum_up = over_rep(g_gate), over_rep(g_up)
    da_pieces = gather_pieces(da_bf)
    da_all = jnp.zeros((groups, count, width), BF)
    for k, piece in enumerate(da_pieces):
        da_all = put(da_all, piece[None], (at[k], zero, zero))
    da_all = da_all.reshape(length, width)
    d_attn = dot_right_t(da_all, o_weight).astype(BF)
    dq, dk, dv = attend_back(queries, keys, values, lse, d_attn)
    dq, dk = turn(dq, cosine, -sine), turn(dk, cosine, -sine)
    q_unit, k_unit = q_proj * q_inv, k_proj * k_inv
    d_q_gain, d_k_gain = jnp.sum(dq * q_unit, axis=0), jnp.sum(dk * k_unit, axis=0)
    dq, dk = dq * gq, dk * gk
    along = jnp.concatenate(
        [jnp.sum(dq * q_unit, axis=1), jnp.sum(dk * k_unit, axis=1), d_attn_gain, d_mlp_gain]
    )
    along = group_sum(along.reshape(-1, 128)).reshape(-1)
    q_mean, k_mean = along[:length, None] / width, along[length : 2 * length, None] / width
    d_qkv = jnp.concatenate(
        [
            (q_inv * (dq - q_unit * q_mean)).astype(BF),
            (k_inv * (dk - k_unit * k_mean)).astype(BF),
            dv.astype(BF),
        ],
        axis=1,
    )
    x_part = dot_right_t(d_qkv, w_qkv).astype(BF)

    g_qkv = dot_left_t(tie(x_all, x_part), d_qkv).astype(BF).reshape(groups, reps, sub, 3 * own)
    g_o = dot_left_t(attn, tie(da_all, dq)).astype(BF).reshape(reps, sub, groups, own)
    g_all = jnp.concatenate([g_qkv, jnp.transpose(g_o, (2, 0, 1, 3))], axis=3)
    parts = [
        lax.dynamic_slice(g_all, (zero, of[j], zero, zero), (groups, 1, sub, 4 * own))[:, 0] for j in range(reps)
    ]
    near = near_send(parts)
    far = far_send(parts, near)
    d_x, last = scatter_sum(
        [lax.dynamic_slice(x_part, (at[k] * count, zero), (count, width)) for k in range(groups)]
    )
    near_place = da_pieces[groups - 4]
    down_grad = to_rows(to_place(sum_down, near_place, d_attn), True)
    gate_grad = to_rows(to_place(sum_gate, near_place, x_part), False)
    up_grad = to_rows(to_place(sum_up, dq, x_part), False)
    sums = rep_total(parts, near, far)
    rows_of = to_columns(tie(sums[..., : 3 * own], *last))
    d_x = d_middle + d_x
    mine = jnp.concatenate([rows_of, sums[..., 3 * own :]], axis=2)
    mine = tie(lax.optimization_barrier(mine), gate_grad)
    far = rep_far(mine)
    here = tie(jnp.stack([mine, far]), down_grad, gate_grad, up_grad)
    q_grad, k_grad, v_grad, o_grad = lay_rows(rep, here, rep_near(here))

    post = lax.dynamic_slice(along[2 * length :].reshape(2, width), (zero, me * own), (2, own))
    gain_sums = jnp.concatenate([jnp.stack([d_q_gain, d_k_gain]), post])
    for step in (1, 2):
        gain_sums = gain_sums + shuffle(gain_sums, "rep", step)
    return (
        outputs[None], d_x.astype(BF)[None], q_grad, k_grad, v_grad, o_grad, gate_grad, up_grad, down_grad,
        gain_sums[0], gain_sums[1], gain_sums[2], gain_sums[3],
    )


def rotary(values, places):
    count = values.shape[0]
    heads = values.reshape(count, HEADS, HEAD)
    freqs = THETA ** (-2.0 * jnp.arange(HEAD // 2, dtype=jnp.float32) / HEAD)
    angles = places[:, None] * freqs[None, :]
    cosine = jnp.cos(angles)[:, None, :]
    sine = jnp.sin(angles)[:, None, :]
    first = heads[..., : HEAD // 2]
    second = heads[..., HEAD // 2 :]
    turned = jnp.concatenate(
        [first * cosine - second * sine, second * cosine + first * sine], axis=-1
    )
    return turned.reshape(count, HEADS * HEAD)


def head_slice(matrix, index):
    piece = lax.dynamic_slice_in_dim(matrix, index * GROUPED * HEAD, GROUPED * HEAD, 1)
    return piece.reshape(matrix.shape[0], GROUPED, HEAD)


def heads_back(stacked, count):
    return jnp.moveaxis(stacked, 0, 1).reshape(count, HEADS * HEAD)


def by_tokens(
    tokens,
    q_weight,
    k_weight,
    v_weight,
    o_weight,
    gate_weight,
    up_weight,
    down_weight,
    q_gain,
    k_gain,
    attn_gain,
    mlp_gain,
    cotangent,
):
    inputs = tokens[0]
    rows = inputs.shape[0]
    width = inputs.shape[1]
    groups = lax.axis_size("grp")
    length = rows * groups
    query_places = lax.axis_index("grp") * rows + jnp.arange(rows, dtype=jnp.int32)
    places = query_places.astype(jnp.float32)
    scale = HEAD ** (-0.5)
    group_ids = jnp.arange(HEADS // GROUPED, dtype=jnp.int32)
    wq_fwd, wk_fwd, wv_fwd, wo_gathered, gq_bf, gk_bf, ga_bf = (
        lax.all_gather(q_weight, "grp", axis=0, tiled=True),
        lax.all_gather(k_weight, "grp", axis=0, tiled=True),
        lax.all_gather(v_weight, "grp", axis=0, tiled=True),
        lax.all_gather(o_weight, "grp", axis=0, tiled=True),
        lax.all_gather(q_gain, "grp", axis=0, tiled=True),
        lax.all_gather(k_gain, "grp", axis=0, tiled=True),
        lax.all_gather(attn_gain, "grp", axis=0, tiled=True),
    )
    gq_full = gq_bf.astype(jnp.float32)
    gk_full = gk_bf.astype(jnp.float32)
    ga_full = ga_bf.astype(jnp.float32)
    q_proj = dot(inputs, wq_fwd)
    k_proj = dot(inputs, wk_fwd)
    v_proj = dot(inputs, wv_fwd)

    def turn_query(values, gains):
        return rotary(rms(values, gains), places)

    queries = turn_query(q_proj, gq_full).astype(jnp.bfloat16)
    keys_own = turn_query(k_proj, gk_full).astype(jnp.bfloat16)
    values_own = v_proj.astype(jnp.bfloat16)
    keys_all, values_all = (
        lax.all_gather(keys_own, "grp", axis=0, tiled=True),
        lax.all_gather(values_own, "grp", axis=0, tiled=True),
    )
    allowed = jnp.arange(length, dtype=jnp.int32)[None, :] <= query_places[:, None]

    def forward_group(index):
        scores = (
            jnp.einsum(
                "qhd,khd->hqk",
                head_slice(queries, index),
                head_slice(keys_all, index),
                preferred_element_type=jnp.float32,
            )
            * scale
        )
        scores = jnp.where(allowed[None], scores, -1e30)
        top_score = jnp.max(scores, axis=-1, keepdims=True)
        weights = jnp.exp(scores - top_score)
        totals = jnp.sum(weights, axis=-1, keepdims=True)
        probs = (weights / totals).astype(jnp.bfloat16)
        mixed = jnp.einsum(
            "hqk,khd->qhd", probs, head_slice(values_all, index), preferred_element_type=jnp.float32
        )
        return (mixed, (top_score + jnp.log(totals))[..., 0])

    mixed_all, log_totals = lax.map(forward_group, group_ids)
    log_totals = log_totals.reshape(HEADS, rows)
    attn_bf = heads_back(mixed_all, rows).astype(jnp.bfloat16)
    a_proj = dot(attn_bf, wo_gathered)
    middle = inputs.astype(jnp.float32) + rms(a_proj, ga_full)
    middle_bf = middle.astype(jnp.bfloat16)
    wg_fwd, wu_fwd, gm_bf = (
        lax.all_gather(gate_weight, "grp", axis=0, tiled=True),
        lax.all_gather(up_weight, "grp", axis=0, tiled=True),
        lax.all_gather(mlp_gain, "grp", axis=0, tiled=True),
    )
    gm_full = gm_bf.astype(jnp.float32)
    gates = dot(middle_bf, wg_fwd)
    uppers = dot(middle_bf, wu_fwd)
    hidden = swiglu(gates, uppers).astype(jnp.bfloat16)
    y_proj = dot(hidden, lax.all_gather(down_weight, "grp", axis=1, tiled=True))
    outputs = (middle + rms(y_proj, gm_full)).astype(jnp.bfloat16)
    grad_out = cotangent[0].astype(jnp.float32)
    unused_y, pull_mlp = jax.vjp(rms, y_proj, gm_full)
    dy_proj, d_mlp_gain = pull_mlp(grad_out)
    dy_bf = dy_proj.astype(jnp.bfloat16)
    down_full = lax.all_gather(down_weight, "grp", axis=1, tiled=True)
    d_hidden = dot_right_t(dy_bf, down_full)
    unused_h, pull_act = jax.vjp(swiglu, gates, uppers)
    d_gates, d_uppers = pull_act(d_hidden)
    dg_bf = d_gates.astype(jnp.bfloat16)
    du_bf = d_uppers.astype(jnp.bfloat16)
    block = dot_right_t(
        dg_bf, lax.all_gather(gate_weight, "grp", axis=0, tiled=True)
    ) + dot_right_t(du_bf, lax.all_gather(up_weight, "grp", axis=0, tiled=True))
    d_middle = grad_out + block
    unused_a, pull_attn = jax.vjp(rms, a_proj, ga_full)
    da_proj, d_attn_gain = pull_attn(d_middle)
    da_bf = da_proj.astype(jnp.bfloat16)
    wq_full, wk_full, wv_full, wo_full = (
        lax.all_gather(q_weight, "grp", axis=0, tiled=True),
        lax.all_gather(k_weight, "grp", axis=0, tiled=True),
        lax.all_gather(v_weight, "grp", axis=0, tiled=True),
        lax.all_gather(o_weight, "grp", axis=0, tiled=True),
    )
    d_attn_bf = dot_right_t(da_bf, wo_full).astype(jnp.bfloat16)

    def query_group(index):
        query_g = head_slice(queries, index)
        key_g = head_slice(keys_all, index)
        dout_g = head_slice(d_attn_bf, index)
        lse_g = lax.dynamic_slice_in_dim(log_totals, index * GROUPED, GROUPED, 0)
        scores = (
            jnp.einsum("qhd,khd->hqk", query_g, key_g, preferred_element_type=jnp.float32) * scale
        )
        scores = jnp.where(allowed[None], scores, -1e30)
        probs = jnp.exp(scores - lse_g[..., None])
        d_probs = jnp.einsum(
            "qhd,khd->hqk",
            dout_g,
            head_slice(values_all, index),
            preferred_element_type=jnp.float32,
        )
        deltas = jnp.sum(probs * d_probs, axis=-1, keepdims=True)
        ds_bf = (probs * (d_probs - deltas)).astype(jnp.bfloat16)
        d_query = (
            jnp.einsum("hqk,khd->qhd", ds_bf, key_g, preferred_element_type=jnp.float32) * scale
        )
        return (d_query, deltas[..., 0])

    d_query_all, delta_all = lax.map(query_group, group_ids)
    d_queries = heads_back(d_query_all, rows)
    delta_all = delta_all.reshape(HEADS, rows)
    key_places = jnp.arange(rows * lax.axis_size("grp"), dtype=jnp.int32)
    permit = key_places[None, :] <= query_places[:, None]

    def key_group(index):
        query_g = head_slice(queries, index)
        dout_g = head_slice(d_attn_bf, index)
        lse_g = lax.dynamic_slice_in_dim(log_totals, index * GROUPED, GROUPED, 0)
        delta_g = lax.dynamic_slice_in_dim(delta_all, index * GROUPED, GROUPED, 0)
        scores = (
            jnp.einsum(
                "qhd,khd->hqk",
                query_g,
                head_slice(keys_all, index),
                preferred_element_type=jnp.float32,
            )
            * scale
        )
        scores = jnp.where(permit[None], scores, -1e30)
        probs = jnp.exp(scores - lse_g[..., None])
        d_value = jnp.einsum(
            "hqk,qhd->khd", probs.astype(jnp.bfloat16), dout_g, preferred_element_type=jnp.float32
        )
        d_probs = jnp.einsum(
            "qhd,khd->hqk",
            dout_g,
            head_slice(values_all, index),
            preferred_element_type=jnp.float32,
        )
        ds_bf = (probs * (d_probs - delta_g[..., None])).astype(jnp.bfloat16)
        d_key = (
            jnp.einsum("hqk,qhd->khd", ds_bf, query_g, preferred_element_type=jnp.float32) * scale
        )
        return (d_key, d_value)

    d_key_all, d_value_all = lax.map(key_group, group_ids)
    key_grads = lax.psum_scatter(
        jnp.concatenate(
            [
                heads_back(d_key_all, rows * lax.axis_size("grp")),
                heads_back(d_value_all, rows * lax.axis_size("grp")),
            ],
            axis=1,
        ),
        "grp",
        scatter_dimension=0,
        tiled=True,
    )
    dv_bf = key_grads[:, width:].astype(jnp.bfloat16)
    unused_q, pull_query = jax.vjp(turn_query, q_proj, gq_full)
    dq_proj, d_q_gain = pull_query(d_queries)
    unused_k, pull_key = jax.vjp(turn_query, k_proj, gk_full)
    dk_proj, d_k_gain = pull_key(key_grads[:, :width])
    dq_bf = dq_proj.astype(jnp.bfloat16)
    dk_bf = dk_proj.astype(jnp.bfloat16)
    d_inputs = (
        d_middle
        + dot_right_t(dq_bf, wq_full)
        + dot_right_t(dk_bf, wk_full)
        + dot_right_t(dv_bf, wv_full)
    )
    owned_rows = width // groups
    pairs = (
        (inputs, dq_bf), (inputs, dk_bf), (inputs, dv_bf), (attn_bf, da_bf),
        (middle_bf, dg_bf), (middle_bf, du_bf), (dy_bf, hidden),
    )
    weight_sums = []
    for left, right in pairs:
        if weight_sums:
            left, right, weight_sums[-1] = lax.optimization_barrier((left, right, weight_sums[-1]))
        share = lax.psum_scatter(dot_left_t(left, right), "grp", scatter_dimension=0, tiled=True)
        weight_sums.append(lax.psum(share, "rep"))
    gain_stack = jnp.stack([d_q_gain, d_k_gain, d_attn_gain, d_mlp_gain])
    gain_total = lax.psum(gain_stack, ("rep", "grp"))
    gain_mine = lax.dynamic_slice_in_dim(
        gain_total, lax.axis_index("grp") * owned_rows, owned_rows, 1
    )
    return (
        outputs[None],
        d_inputs.astype(jnp.bfloat16)[None],
        *weight_sums[:6],
        weight_sums[6].T,
        gain_mine[0],
        gain_mine[1],
        gain_mine[2],
        gain_mine[3],
    )


def solution(mesh):
    rows = P("grp", None)
    seq = P("rep", "grp", None)
    gain = P("grp")
    whole_heads = HEADS % mesh.shape["grp"] == 0 and mesh.shape["grp"] >= 4 and mesh.shape["rep"] == 4
    return jax.shard_map(
        by_heads if whole_heads else by_tokens,
        mesh=mesh,
        in_specs=(seq, *[rows] * 6, P(None, "grp"), *[gain] * 4, seq),
        out_specs=(seq, seq, *[rows] * 6, P(None, "grp"), *[gain] * 4),
        check_vma=False,
    )
```

```python
import jax
import jax.numpy as jnp
from jax import lax
from jax.experimental import pallas as pl
from jax.experimental.pallas import tpu as pltpu
from jax.sharding import PartitionSpec as P

HEADS = 16
HEAD = 128
EPS = 1e-06
THETA = 500000.0
GROUPED = 4
BF = jnp.bfloat16
F32 = jnp.float32


def dot(left, right, dims=((1,), (0,)), kind=F32):
    return lax.dot_general(left, right, (dims, ((), ())), preferred_element_type=kind)


def dot_right_t(left, right):
    return dot(left, right, ((1,), (1,)))


def dot_left_t(left, right):
    return dot(left, right, ((0,), (0,)))


def shuffle(value, axis, step):
    return lax.ppermute(value, axis, [(i, i ^ step) for i in range(lax.axis_size(axis))])


def tie(value, *others):
    return lax.optimization_barrier((value, *others))[0]


def gather_pieces(value, *meanwhile):
    count = lax.axis_size("grp")
    top = count - 2
    pieces = [None] * count
    pieces[0] = value
    pieces[top] = shuffle(value, "grp", top)
    for step in range(2, count // 2, 2):
        pieces[step] = shuffle(value, "grp", step)
    pieces[1] = shuffle(value, "grp", 1)
    for step in range(count // 2, top, 2):
        pieces[step] = shuffle(pieces[top], "grp", step ^ top)
    steps = [*range(2, count // 2, 2), top, *range(count // 2, top, 2)]
    for step in steps:
        held = meanwhile if step == steps[-1] else ()
        pieces[step + 1] = shuffle(tie(pieces[step], *held) if held else pieces[step], "grp", 1)
    return pieces


def scatter_sum(pieces, *meanwhile):
    count = len(pieces)
    top = count - 2
    odd = {k: shuffle(pieces[k + 1].astype(BF), "grp", 1) for k in range(count // 2, top, 2)}
    odd |= {k: shuffle(pieces[k + 1].astype(BF), "grp", 1) for k in (top, *range(2, count // 2, 2), 0)}
    paired = {k: pieces[k].astype(F32) + odd[k].astype(F32) for k in range(count // 2, top, 2)}
    passed = [shuffle(v.astype(BF), "grp", k ^ top) for k, v in paired.items()]
    held = tie(odd[top], *passed) if passed else odd[top]
    farthest = pieces[top].astype(F32) + held.astype(F32) + sum(v.astype(F32) for v in passed)
    farthest = shuffle(farthest.astype(BF), "grp", top)
    total = pieces[0].astype(F32)
    last = []
    for k in range(2, count // 2, 2):
        held = tie(odd[k], *passed, *meanwhile)
        last.append(shuffle((pieces[k].astype(F32) + held.astype(F32)).astype(BF), "grp", k))
        total += last[-1].astype(F32)
    return total + farthest.astype(F32) + odd[0].astype(F32), last


def to_columns(blocks):
    return lax.all_to_all(blocks, "grp", 0, 0, tiled=True)


def group_sum(value):
    step = 1
    while step < lax.axis_size("grp"):
        value = value + shuffle(value, "grp", step)
        step *= 2
    return value


def rep_near(value):
    return shuffle(value, "rep", 1)


def rep_far(value):
    return shuffle(value, "rep", 2)


def near_send(parts):
    return rep_near(jnp.stack([parts[1], parts[3]]))


def far_send(parts, near):
    return rep_far((parts[2].astype(F32) + near[1].astype(F32)).astype(BF))


def rep_total(parts, near, far):
    return (parts[0].astype(F32) + near[0].astype(F32) + far.astype(F32)).astype(BF)


def lay_kernel(rep_ref, here_ref, there_ref, *out_refs):
    del rep_ref
    wide = here_ref.shape[3] // len(out_refs)
    here = pl.program_id(0) % 2 == 0
    for i, out_ref in enumerate(out_refs):
        for g in range(here_ref.shape[1]):
            piece = jnp.where(
                here,
                here_ref[0, g, :, i * wide : (i + 1) * wide].astype(F32),
                there_ref[0, g, :, i * wide : (i + 1) * wide].astype(F32),
            )
            out_ref[:, g * wide : (g + 1) * wide] = piece


def lay_rows(rep, here, there):
    _, groups, rows, wide = here.shape
    width = groups * wide // 4
    half = rows // 2
    spec = pl.BlockSpec((1, groups, half, wide), lambda j, h, rep_ref: (j // 2, 0, h, 0))
    out = pl.BlockSpec((half, width), lambda j, h, rep_ref: ((rep_ref[0] ^ j) * 2 + h, 0))
    return pl.pallas_call(
        lay_kernel,
        grid_spec=pltpu.PrefetchScalarGridSpec(
            num_scalar_prefetch=1, grid=(4, 2), in_specs=[spec, spec], out_specs=[out] * 4
        ),
        out_shape=[jax.ShapeDtypeStruct((4 * rows, width), F32)] * 4,
        cost_estimate=pl.CostEstimate(flops=0, bytes_accessed=here.size * 12, transcendentals=0),
    )(rep[None], here, there)


def cut_kernel(rep_ref, gate_ref, up_ref, down_ref, gate_out, up_out, down_out):
    del rep_ref
    gate_out[0] = gate_ref[...]
    up_out[0] = up_ref[...]
    down_out[0] = down_ref[...].T


def cut(rep, gate, up, down, groups, reps):
    rows, part = gate.shape[0], gate.shape[1] // (groups * reps)
    wide = pl.BlockSpec((rows, part), lambda g, rep_ref: (0, g * reps + rep_ref[0]))
    tall = pl.BlockSpec((part, rows), lambda g, rep_ref: (g * reps + rep_ref[0], 0))
    out = pl.BlockSpec((1, rows, part), lambda g, rep_ref: (g, 0, 0))
    return pl.pallas_call(
        cut_kernel,
        grid_spec=pltpu.PrefetchScalarGridSpec(
            num_scalar_prefetch=1, grid=(groups,), in_specs=[wide, wide, tall], out_specs=[out] * 3
        ),
        out_shape=[jax.ShapeDtypeStruct((groups, rows, part), BF)] * 3,
        cost_estimate=pl.CostEstimate(flops=0, bytes_accessed=groups * rows * part * 12, transcendentals=0),
    )(rep[None], gate, up, down)


def widen_kernel(x_ref, o_ref):
    for r in range(x_ref.shape[0]):
        wide = x_ref.shape[3]
        o_ref[:, r * wide : (r + 1) * wide] = x_ref[r, 0].astype(F32)


def widen_turned_kernel(x_ref, o_ref):
    for r in range(x_ref.shape[0]):
        tall = x_ref.shape[3]
        o_ref[r * tall : (r + 1) * tall, :] = x_ref[r, 0].astype(F32).T


def widen(parts, turned):
    reps, count, rows, wide = parts.shape
    half = rows // 2
    out = (half, reps * wide) if not turned else (reps * wide, half)
    full = (rows, reps * count * wide) if not turned else (reps * count * wide, rows)
    return pl.pallas_call(
        widen_turned_kernel if turned else widen_kernel,
        grid=(count, 2),
        in_specs=[pl.BlockSpec((reps, 1, half, wide), lambda s, h: (0, s, h, 0))],
        out_specs=pl.BlockSpec(out, (lambda s, h: (s, h)) if turned else (lambda s, h: (h, s))),
        out_shape=jax.ShapeDtypeStruct(full, F32),
        cost_estimate=pl.CostEstimate(flops=0, bytes_accessed=parts.size * 6, transcendentals=0),
    )(parts)


def put(buffer, part, starts):
    return lax.dynamic_update_slice(buffer, part, starts)


def rms(values, gains):
    return values * lax.rsqrt(jnp.mean(values * values, axis=-1, keepdims=True) + EPS) * gains


def angles_of(count):
    freqs = THETA ** (-2.0 * jnp.arange(HEAD // 2, dtype=F32) / HEAD)
    angles = jnp.arange(count, dtype=jnp.int32).astype(F32)[:, None] * freqs[None, :]
    return jnp.cos(angles), jnp.sin(angles)


def turn(values, cosine, sine):
    half = HEAD // 2
    out = []
    for start in range(0, values.shape[1], HEAD):
        first, second = values[:, start : start + half], values[:, start + half : start + HEAD]
        out += [first * cosine - second * sine, second * cosine + first * sine]
    return jnp.concatenate(out, axis=1)


def swiglu(gates, uppers):
    return jax.nn.silu(gates) * uppers


def attend(queries, keys, values):
    length = queries.shape[0]
    split = lambda a: a.reshape(length, -1, HEAD)
    scores = jnp.einsum("qhd,khd->hqk", split(queries), split(keys), preferred_element_type=F32)
    scores = scores * HEAD ** (-0.5)
    places = jnp.arange(length, dtype=jnp.int32)
    scores = jnp.where((places[None, :] <= places[:, None])[None], scores, -1e30)
    top = jnp.max(scores, axis=-1, keepdims=True)
    weights = jnp.exp(scores - top)
    totals = jnp.sum(weights, axis=-1, keepdims=True)
    probs = (weights / totals).astype(BF)
    mixed = jnp.einsum("hqk,khd->qhd", probs, split(values), preferred_element_type=F32)
    return mixed.reshape(length, -1).astype(BF), top + jnp.log(totals)


def attend_back(queries, keys, values, lse, grads):
    length = queries.shape[0]
    split = lambda a: a.reshape(length, -1, HEAD)
    scale = HEAD ** (-0.5)
    q, k, v, do = split(queries), split(keys), split(values), split(grads)
    scores = jnp.einsum("qhd,khd->hqk", q, k, preferred_element_type=F32) * scale
    places = jnp.arange(length, dtype=jnp.int32)
    scores = jnp.where((places[None, :] <= places[:, None])[None], scores, -1e30)
    probs = jnp.exp(scores - lse)
    d_probs = jnp.einsum("qhd,khd->hqk", do, v, preferred_element_type=F32)
    delta = jnp.sum(probs * d_probs, axis=-1, keepdims=True)
    ds = (probs * (d_probs - delta)).astype(BF)
    dv = jnp.einsum("hqk,qhd->khd", probs.astype(BF), do, preferred_element_type=F32)
    dq = jnp.einsum("hqk,khd->qhd", ds, k, preferred_element_type=F32) * scale
    dk = jnp.einsum("hqk,qhd->khd", ds, q, preferred_element_type=F32) * scale
    return dq.reshape(length, -1), dk.reshape(length, -1), dv.reshape(length, -1)


def by_heads(
    tokens, q_weight, k_weight, v_weight, o_weight, gate_weight, up_weight, down_weight,
    q_gain, k_gain, attn_gain, mlp_gain, cotangent,
):
    x = tokens[0]
    count, width = x.shape
    groups = lax.axis_size("grp")
    reps = 4
    me, rep = lax.axis_index("grp"), lax.axis_index("rep")
    length = count * groups
    own = width // groups
    hidden = gate_weight.shape[1]
    block = hidden // groups
    part = block // reps
    sub = own // reps
    zero = jnp.int32(0)
    at = [me ^ k for k in range(groups)]
    of = [rep ^ j for j in range(reps)]

    qkv_rows = jnp.concatenate(
        [
            lax.dynamic_slice(w, (rep * sub, zero), (sub, width)).reshape(sub, groups, own)
            for w in (q_weight, k_weight, v_weight)
        ],
        axis=2,
    )
    gains = jnp.pad(jnp.concatenate([attn_gain, mlp_gain])[None], ((0, 7), (0, own)))
    gains = jnp.broadcast_to(gains[None], (groups, 8, 3 * own))
    landed = to_columns(jnp.concatenate([jnp.transpose(qkv_rows, (1, 0, 2)), gains], axis=1))
    gain_all = landed[:, sub, : 2 * own].astype(F32).reshape(groups, 2, own)
    ga, gm = gain_all[:, 0].reshape(width), gain_all[:, 1].reshape(width)
    mine = landed[:, :sub]
    far = rep_far(mine)
    x_pieces = gather_pieces(x)
    near = rep_near(jnp.stack([mine, far]))
    w_qkv = jnp.zeros((groups, reps, sub, 3 * own), BF)
    for j, piece in enumerate([mine, near[0], far, near[1]]):
        w_qkv = put(w_qkv, piece[:, None], (zero, of[j], zero, zero))
    w_qkv = w_qkv.reshape(width, 3 * own)

    x_all = jnp.zeros((groups, count, width), BF)
    for k, piece in enumerate(x_pieces):
        x_all = put(x_all, piece[None], (at[k], zero, zero))
    x_all = x_all.reshape(length, width)

    sends = cut(rep, gate_weight, up_weight, down_weight, groups, reps)

    def spread(blocks):
        return lax.all_gather(blocks.reshape(width, part), "rep", axis=1, tiled=True)

    gq, gk = q_gain.astype(F32), k_gain.astype(F32)
    cosine, sine = angles_of(length)
    qkv = dot(x_all, w_qkv)
    q_proj, k_proj = qkv[:, :own], qkv[:, own : 2 * own]
    values = qkv[:, 2 * own :].astype(BF)
    squares = jnp.stack([jnp.sum(q_proj * q_proj, axis=1), jnp.sum(k_proj * k_proj, axis=1)])
    squares = group_sum(squares)
    q_inv = lax.rsqrt(squares[0] / width + EPS)[:, None]
    k_inv = lax.rsqrt(squares[1] / width + EPS)[:, None]
    queries = turn(q_proj * q_inv * gq, cosine, sine).astype(BF)
    keys = turn(k_proj * k_inv * gk, cosine, sine).astype(BF)
    attn, lse = attend(queries, keys, values)
    gu_landed = tie(to_columns(tie(jnp.concatenate(sends[:2], axis=2), x_pieces[groups - 1])), squares)
    w_gate, w_up = spread(gu_landed[..., :part]), spread(gu_landed[..., part:])
    a_part = dot(attn, o_weight).astype(BF)
    a_proj, _ = scatter_sum(
        [lax.dynamic_slice(a_part, (at[k] * count, zero), (count, width)) for k in range(groups)]
    )
    w_down = spread(tie(to_columns(tie(sends[2], gu_landed)), attn))
    middle = x.astype(F32) + rms(a_proj, ga)
    middle_bf = middle.astype(BF)

    def halves(pieces):
        return jnp.concatenate(pieces[0::2]), jnp.concatenate(pieces[1::2])

    def whole(*parts):
        parts = [v.reshape(-1, count, width) for v in parts]
        return [parts[k % len(parts)][k // len(parts)] for k in range(groups)]

    h_halves = halves(gather_pieces(middle_bf, w_gate))
    gates = [dot(h, w_gate) for h in h_halves]
    uppers = [dot(h, w_up) for h in h_halves]
    mixed = [swiglu(g, u).astype(BF) for g, u in zip(gates, uppers)]
    y_proj, _ = scatter_sum(whole(*[dot_right_t(m, w_down).astype(BF) for m in mixed]))
    outputs = (middle + rms(y_proj, gm)).astype(BF)

    grad_out = cotangent[0].astype(F32)
    _, pull = jax.vjp(rms, y_proj, gm)
    dy, d_mlp_gain = pull(grad_out)
    dy_pieces = gather_pieces(dy.astype(BF))
    dy_halves = halves([tie(dy_pieces[0], dy_pieces[groups - 1]), *dy_pieces[1:]])
    d_gates, d_uppers, m_halves = [], [], []
    for g, u, d in zip(gates, uppers, dy_halves):
        _, pull = jax.vjp(swiglu, g, u)
        d_gate, d_upper = (v.astype(BF) for v in pull(dot(d, w_down)))
        d_gates.append(d_gate)
        d_uppers.append(d_upper)
        m_halves.append((dot_right_t(d_gate, w_gate) + dot_right_t(d_upper, w_up)).astype(BF))
    d_middle, _ = scatter_sum(whole(*m_halves))
    d_middle = grad_out + d_middle

    def weight_part(left, right):
        return sum(dot_left_t(a, b) for a, b in zip(left, right)).astype(BF)

    def over_rep(part_sum):
        return lax.psum_scatter(part_sum, "rep", scatter_dimension=1, tiled=True)

    def to_place(sums, before, after):
        return tie(to_columns(tie(sums.reshape(groups, own, part), before)), after)

    def to_rows(sums, turned):
        return widen(lax.all_gather(lax.optimization_barrier(sums), "rep", axis=0), turned)

    g_down = weight_part(dy_halves, mixed)
    g_gate, g_up = weight_part(h_halves, d_gates), weight_part(h_halves, d_uppers)
    sum_down = over_rep(tie(g_down, *m_halves))
    d_middle = tie(d_middle, sum_down, g_gate, g_up)
    _, pull = jax.vjp(rms, a_proj, ga)
    da, d_attn_gain = pull(d_middle)
    da_bf = da.astype(BF)
    sum_gate, sum_up = over_rep(g_gate), over_rep(g_up)
    da_pieces = gather_pieces(da_bf)
    da_all = jnp.zeros((groups, count, width), BF)
    for k, piece in enumerate(da_pieces):
        da_all = put(da_all, piece[None], (at[k], zero, zero))
    da_all = da_all.reshape(length, width)
    d_attn = dot_right_t(da_all, o_weight).astype(BF)
    dq, dk, dv = attend_back(queries, keys, values, lse, d_attn)
    dq, dk = turn(dq, cosine, -sine), turn(dk, cosine, -sine)
    q_unit, k_unit = q_proj * q_inv, k_proj * k_inv
    d_q_gain, d_k_gain = jnp.sum(dq * q_unit, axis=0), jnp.sum(dk * k_unit, axis=0)
    dq, dk = dq * gq, dk * gk
    along = jnp.concatenate(
        [jnp.sum(dq * q_unit, axis=1), jnp.sum(dk * k_unit, axis=1), d_attn_gain, d_mlp_gain]
    )
    along = group_sum(along.reshape(-1, 128)).reshape(-1)
    q_mean, k_mean = along[:length, None] / width, along[length : 2 * length, None] / width
    d_qkv = jnp.concatenate(
        [
            (q_inv * (dq - q_unit * q_mean)).astype(BF),
            (k_inv * (dk - k_unit * k_mean)).astype(BF),
            dv.astype(BF),
        ],
        axis=1,
    )
    x_part = dot_right_t(d_qkv, w_qkv).astype(BF)

    g_qkv = dot_left_t(tie(x_all, x_part), d_qkv).astype(BF).reshape(groups, reps, sub, 3 * own)
    g_o = dot_left_t(attn, tie(da_all, dq)).astype(BF).reshape(reps, sub, groups, own)
    g_all = jnp.concatenate([g_qkv, jnp.transpose(g_o, (2, 0, 1, 3))], axis=3)
    parts = [
        lax.dynamic_slice(g_all, (zero, of[j], zero, zero), (groups, 1, sub, 4 * own))[:, 0] for j in range(reps)
    ]
    near = near_send(parts)
    far = far_send(parts, near)
    d_x, last = scatter_sum(
        [lax.dynamic_slice(x_part, (at[k] * count, zero), (count, width)) for k in range(groups)]
    )
    near_place = da_pieces[groups - 4]
    down_grad = to_rows(to_place(sum_down, near_place, d_attn), True)
    gate_grad = to_rows(to_place(sum_gate, near_place, x_part), False)
    up_grad = to_rows(to_place(sum_up, dq, x_part), False)
    sums = rep_total(parts, near, far)
    rows_of = to_columns(tie(sums[..., : 3 * own], *last))
    d_x = d_middle + d_x
    mine = jnp.concatenate([rows_of, sums[..., 3 * own :]], axis=2)
    mine = tie(lax.optimization_barrier(mine), gate_grad)
    far = rep_far(mine)
    here = tie(jnp.stack([mine, far]), down_grad, gate_grad, up_grad)
    q_grad, k_grad, v_grad, o_grad = lay_rows(rep, here, rep_near(here))

    post = lax.dynamic_slice(along[2 * length :].reshape(2, width), (zero, me * own), (2, own))
    gain_sums = jnp.concatenate([jnp.stack([d_q_gain, d_k_gain]), post])
    for step in (1, 2):
        gain_sums = gain_sums + shuffle(gain_sums, "rep", step)
    return (
        outputs[None], d_x.astype(BF)[None], q_grad, k_grad, v_grad, o_grad, gate_grad, up_grad, down_grad,
        gain_sums[0], gain_sums[1], gain_sums[2], gain_sums[3],
    )


def rotary(values, places):
    count = values.shape[0]
    heads = values.reshape(count, HEADS, HEAD)
    freqs = THETA ** (-2.0 * jnp.arange(HEAD // 2, dtype=jnp.float32) / HEAD)
    angles = places[:, None] * freqs[None, :]
    cosine = jnp.cos(angles)[:, None, :]
    sine = jnp.sin(angles)[:, None, :]
    first = heads[..., : HEAD // 2]
    second = heads[..., HEAD // 2 :]
    turned = jnp.concatenate(
        [first * cosine - second * sine, second * cosine + first * sine], axis=-1
    )
    return turned.reshape(count, HEADS * HEAD)


def head_slice(matrix, index):
    piece = lax.dynamic_slice_in_dim(matrix, index * GROUPED * HEAD, GROUPED * HEAD, 1)
    return piece.reshape(matrix.shape[0], GROUPED, HEAD)


def heads_back(stacked, count):
    return jnp.moveaxis(stacked, 0, 1).reshape(count, HEADS * HEAD)


def by_tokens(
    tokens,
    q_weight,
    k_weight,
    v_weight,
    o_weight,
    gate_weight,
    up_weight,
    down_weight,
    q_gain,
    k_gain,
    attn_gain,
    mlp_gain,
    cotangent,
):
    inputs = tokens[0]
    rows = inputs.shape[0]
    width = inputs.shape[1]
    groups = lax.axis_size("grp")
    length = rows * groups
    query_places = lax.axis_index("grp") * rows + jnp.arange(rows, dtype=jnp.int32)
    places = query_places.astype(jnp.float32)
    scale = HEAD ** (-0.5)
    group_ids = jnp.arange(HEADS // GROUPED, dtype=jnp.int32)
    wq_fwd, wk_fwd, wv_fwd, wo_gathered, gq_bf, gk_bf, ga_bf = (
        lax.all_gather(q_weight, "grp", axis=0, tiled=True),
        lax.all_gather(k_weight, "grp", axis=0, tiled=True),
        lax.all_gather(v_weight, "grp", axis=0, tiled=True),
        lax.all_gather(o_weight, "grp", axis=0, tiled=True),
        lax.all_gather(q_gain, "grp", axis=0, tiled=True),
        lax.all_gather(k_gain, "grp", axis=0, tiled=True),
        lax.all_gather(attn_gain, "grp", axis=0, tiled=True),
    )
    gq_full = gq_bf.astype(jnp.float32)
    gk_full = gk_bf.astype(jnp.float32)
    ga_full = ga_bf.astype(jnp.float32)
    q_proj = dot(inputs, wq_fwd)
    k_proj = dot(inputs, wk_fwd)
    v_proj = dot(inputs, wv_fwd)

    def turn_query(values, gains):
        return rotary(rms(values, gains), places)

    queries = turn_query(q_proj, gq_full).astype(jnp.bfloat16)
    keys_own = turn_query(k_proj, gk_full).astype(jnp.bfloat16)
    values_own = v_proj.astype(jnp.bfloat16)
    keys_all, values_all = (
        lax.all_gather(keys_own, "grp", axis=0, tiled=True),
        lax.all_gather(values_own, "grp", axis=0, tiled=True),
    )
    allowed = jnp.arange(length, dtype=jnp.int32)[None, :] <= query_places[:, None]

    def forward_group(index):
        scores = (
            jnp.einsum(
                "qhd,khd->hqk",
                head_slice(queries, index),
                head_slice(keys_all, index),
                preferred_element_type=jnp.float32,
            )
            * scale
        )
        scores = jnp.where(allowed[None], scores, -1e30)
        top_score = jnp.max(scores, axis=-1, keepdims=True)
        weights = jnp.exp(scores - top_score)
        totals = jnp.sum(weights, axis=-1, keepdims=True)
        probs = (weights / totals).astype(jnp.bfloat16)
        mixed = jnp.einsum(
            "hqk,khd->qhd", probs, head_slice(values_all, index), preferred_element_type=jnp.float32
        )
        return (mixed, (top_score + jnp.log(totals))[..., 0])

    mixed_all, log_totals = lax.map(forward_group, group_ids)
    log_totals = log_totals.reshape(HEADS, rows)
    attn_bf = heads_back(mixed_all, rows).astype(jnp.bfloat16)
    a_proj = dot(attn_bf, wo_gathered)
    middle = inputs.astype(jnp.float32) + rms(a_proj, ga_full)
    middle_bf = middle.astype(jnp.bfloat16)
    wg_fwd, wu_fwd, gm_bf = (
        lax.all_gather(gate_weight, "grp", axis=0, tiled=True),
        lax.all_gather(up_weight, "grp", axis=0, tiled=True),
        lax.all_gather(mlp_gain, "grp", axis=0, tiled=True),
    )
    gm_full = gm_bf.astype(jnp.float32)
    gates = dot(middle_bf, wg_fwd)
    uppers = dot(middle_bf, wu_fwd)
    hidden = swiglu(gates, uppers).astype(jnp.bfloat16)
    y_proj = dot(hidden, lax.all_gather(down_weight, "grp", axis=1, tiled=True))
    outputs = (middle + rms(y_proj, gm_full)).astype(jnp.bfloat16)
    grad_out = cotangent[0].astype(jnp.float32)
    unused_y, pull_mlp = jax.vjp(rms, y_proj, gm_full)
    dy_proj, d_mlp_gain = pull_mlp(grad_out)
    dy_bf = dy_proj.astype(jnp.bfloat16)
    down_full = lax.all_gather(down_weight, "grp", axis=1, tiled=True)
    d_hidden = dot_right_t(dy_bf, down_full)
    unused_h, pull_act = jax.vjp(swiglu, gates, uppers)
    d_gates, d_uppers = pull_act(d_hidden)
    dg_bf = d_gates.astype(jnp.bfloat16)
    du_bf = d_uppers.astype(jnp.bfloat16)
    block = dot_right_t(
        dg_bf, lax.all_gather(gate_weight, "grp", axis=0, tiled=True)
    ) + dot_right_t(du_bf, lax.all_gather(up_weight, "grp", axis=0, tiled=True))
    d_middle = grad_out + block
    unused_a, pull_attn = jax.vjp(rms, a_proj, ga_full)
    da_proj, d_attn_gain = pull_attn(d_middle)
    da_bf = da_proj.astype(jnp.bfloat16)
    wq_full, wk_full, wv_full, wo_full = (
        lax.all_gather(q_weight, "grp", axis=0, tiled=True),
        lax.all_gather(k_weight, "grp", axis=0, tiled=True),
        lax.all_gather(v_weight, "grp", axis=0, tiled=True),
        lax.all_gather(o_weight, "grp", axis=0, tiled=True),
    )
    d_attn_bf = dot_right_t(da_bf, wo_full).astype(jnp.bfloat16)

    def query_group(index):
        query_g = head_slice(queries, index)
        key_g = head_slice(keys_all, index)
        dout_g = head_slice(d_attn_bf, index)
        lse_g = lax.dynamic_slice_in_dim(log_totals, index * GROUPED, GROUPED, 0)
        scores = (
            jnp.einsum("qhd,khd->hqk", query_g, key_g, preferred_element_type=jnp.float32) * scale
        )
        scores = jnp.where(allowed[None], scores, -1e30)
        probs = jnp.exp(scores - lse_g[..., None])
        d_probs = jnp.einsum(
            "qhd,khd->hqk",
            dout_g,
            head_slice(values_all, index),
            preferred_element_type=jnp.float32,
        )
        deltas = jnp.sum(probs * d_probs, axis=-1, keepdims=True)
        ds_bf = (probs * (d_probs - deltas)).astype(jnp.bfloat16)
        d_query = (
            jnp.einsum("hqk,khd->qhd", ds_bf, key_g, preferred_element_type=jnp.float32) * scale
        )
        return (d_query, deltas[..., 0])

    d_query_all, delta_all = lax.map(query_group, group_ids)
    d_queries = heads_back(d_query_all, rows)
    delta_all = delta_all.reshape(HEADS, rows)
    key_places = jnp.arange(rows * lax.axis_size("grp"), dtype=jnp.int32)
    permit = key_places[None, :] <= query_places[:, None]

    def key_group(index):
        query_g = head_slice(queries, index)
        dout_g = head_slice(d_attn_bf, index)
        lse_g = lax.dynamic_slice_in_dim(log_totals, index * GROUPED, GROUPED, 0)
        delta_g = lax.dynamic_slice_in_dim(delta_all, index * GROUPED, GROUPED, 0)
        scores = (
            jnp.einsum(
                "qhd,khd->hqk",
                query_g,
                head_slice(keys_all, index),
                preferred_element_type=jnp.float32,
            )
            * scale
        )
        scores = jnp.where(permit[None], scores, -1e30)
        probs = jnp.exp(scores - lse_g[..., None])
        d_value = jnp.einsum(
            "hqk,qhd->khd", probs.astype(jnp.bfloat16), dout_g, preferred_element_type=jnp.float32
        )
        d_probs = jnp.einsum(
            "qhd,khd->hqk",
            dout_g,
            head_slice(values_all, index),
            preferred_element_type=jnp.float32,
        )
        ds_bf = (probs * (d_probs - delta_g[..., None])).astype(jnp.bfloat16)
        d_key = (
            jnp.einsum("hqk,qhd->khd", ds_bf, query_g, preferred_element_type=jnp.float32) * scale
        )
        return (d_key, d_value)

    d_key_all, d_value_all = lax.map(key_group, group_ids)
    key_grads = lax.psum_scatter(
        jnp.concatenate(
            [
                heads_back(d_key_all, rows * lax.axis_size("grp")),
                heads_back(d_value_all, rows * lax.axis_size("grp")),
            ],
            axis=1,
        ),
        "grp",
        scatter_dimension=0,
        tiled=True,
    )
    dv_bf = key_grads[:, width:].astype(jnp.bfloat16)
    unused_q, pull_query = jax.vjp(turn_query, q_proj, gq_full)
    dq_proj, d_q_gain = pull_query(d_queries)
    unused_k, pull_key = jax.vjp(turn_query, k_proj, gk_full)
    dk_proj, d_k_gain = pull_key(key_grads[:, :width])
    dq_bf = dq_proj.astype(jnp.bfloat16)
    dk_bf = dk_proj.astype(jnp.bfloat16)
    d_inputs = (
        d_middle
        + dot_right_t(dq_bf, wq_full)
        + dot_right_t(dk_bf, wk_full)
        + dot_right_t(dv_bf, wv_full)
    )
    owned_rows = width // groups
    pairs = (
        (inputs, dq_bf), (inputs, dk_bf), (inputs, dv_bf), (attn_bf, da_bf),
        (middle_bf, dg_bf), (middle_bf, du_bf), (dy_bf, hidden),
    )
    weight_sums = []
    for left, right in pairs:
        if weight_sums:
            left, right, weight_sums[-1] = lax.optimization_barrier((left, right, weight_sums[-1]))
        share = lax.psum_scatter(dot_left_t(left, right), "grp", scatter_dimension=0, tiled=True)
        weight_sums.append(lax.psum(share, "rep"))
    gain_stack = jnp.stack([d_q_gain, d_k_gain, d_attn_gain, d_mlp_gain])
    gain_total = lax.psum(gain_stack, ("rep", "grp"))
    gain_mine = lax.dynamic_slice_in_dim(
        gain_total, lax.axis_index("grp") * owned_rows, owned_rows, 1
    )
    return (
        outputs[None],
        d_inputs.astype(jnp.bfloat16)[None],
        *weight_sums[:6],
        weight_sums[6].T,
        gain_mine[0],
        gain_mine[1],
        gain_mine[2],
        gain_mine[3],
    )


def solution(mesh):
    rows = P("grp", None)
    seq = P("rep", "grp", None)
    gain = P("grp")
    whole_heads = HEADS % mesh.shape["grp"] == 0 and mesh.shape["grp"] >= 4 and mesh.shape["rep"] == 4
    return jax.shard_map(
        by_heads if whole_heads else by_tokens,
        mesh=mesh,
        in_specs=(seq, *[rows] * 6, P(None, "grp"), *[gain] * 4, seq),
        out_specs=(seq, seq, *[rows] * 6, P(None, "grp"), *[gain] * 4),
        check_vma=False,
    )
```
